256 devices in a mesh: segment: 4 (over x), tm: 2 (over core), space: 32 (over z, y).
Axes of the slice: x: 4, y: 4, z: 8, core: 2. Of those that a mesh axis runs over, the one named last changes fastest.
Arguments:
- inputs: bfloat16 [4, 8, 256, 16, 128], P(None, 'tm', 'space'), may hold values from -6 to 6
- weights: bfloat16 [4, 3456, 128], P('segment'), may hold values from -0.109375 to 0.109375
- cotangent: bfloat16 [4, 8, 256, 16, 128], P(None, 'tm', 'space'), may hold values from -0.023925781 to 0.023925781
Outputs:
- weight_grads: float32 [4, 3456, 128], P('segment')
The draws below stay inside these ranges and needn't reach their ends.
All inputs are finite; a program needn't handle non-finite values.
Results may differ from the reference program's by a relative error of at most 0.009.
Values may be sent and summed in bfloat16 or wider, within the bound.
No kernel may reach another device: no remote copies, remote signals or barrier semaphores. Data moves between devices by JAX's collectives and lax.ppermute only.
A program may use at most 64 MiB of HBM per device.

```python
import jax
import jax.numpy as jnp
from jax import lax

C = 128
COLS = 16
MICRO = 4
LAYERS = 4
KC = 3456
FRAMES = 8
ROWS = 256


def block_levels(stream_key, shape, split, smallest, top_value):
    factor_of, own = 1.0, jax.random.fold_in(stream_key, 6)
    for axis_at, blocks in split:
        draws = jnp.exp(jax.random.uniform(jax.random.fold_in(own, axis_at), (blocks,), jnp.float32, smallest / len(split), top_value / len(split)))
        factor_of = factor_of * jnp.repeat(draws, shape[axis_at] // blocks).reshape([-1 if axis == axis_at else 1 for axis in range(len(shape))])
    return factor_of


def bell_draw(own_key, extent, deviation, reach, split=(), held_as=jnp.bfloat16):
    drawn = jax.random.normal(own_key, extent, jnp.float32) * deviation
    if len(split) > 0:
        drawn = block_levels(own_key, extent, split, -0.22, 0.18) * drawn
    return jnp.clip(drawn, min=-reach, max=reach).astype(held_as)


def setup_inputs(seed: int = 0) -> dict:
    key_list = jax.random.split(jax.random.key(seed), 4)
    return {
        "inputs": bell_draw(key_list[0], (MICRO, FRAMES, ROWS, COLS, C), 1.0, 6.0, ((1, 2), (2, 32))),
        "weights": bell_draw(key_list[1], (LAYERS, KC, C), KC ** -0.5, 0.109375, ((0, 4),)),
        "cotangent": bell_draw(key_list[2], (MICRO, FRAMES, ROWS, COLS, C), 0.004, 0.023925781, ((1, 2), (2, 32))),
    }


def taps(extended, frame_count, row_count, col_count, flipped):
    pieces = []
    for lag_t in range(3):
        for lag_r in range(3):
            for lag_c in range(3):
                if flipped:
                    start_t, start_r, start_c = 2 - lag_t, 2 - lag_r, 2 - lag_c
                else:
                    start_t, start_r, start_c = lag_t, lag_r, lag_c
                pieces.append(extended[start_t:start_t + frame_count, start_r:start_r + row_count, start_c:start_c + col_count])
    joined = jnp.concatenate(pieces, -1)
    return joined.reshape(frame_count * row_count * col_count, -1)


def reference(inputs, weights, cotangent):
    frame_count, row_count, col_count, channels = inputs.shape[1:]
    layer_count = weights.shape[0]
    cells = frame_count * row_count * col_count
    weight_grads = [jnp.zeros((weights.shape[1], channels), jnp.float32) for layer_idx in range(layer_count)]
    for sample in range(inputs.shape[0]):
        hidden = inputs[sample]
        stored = []
        for layer_idx in range(layer_count):
            extended = jnp.pad(hidden, ((2, 0), (1, 1), (1, 1), (0, 0)))
            stored.append(extended)
            pre_act = jnp.dot(taps(extended, frame_count, row_count, col_count, False), weights[layer_idx], preferred_element_type=jnp.float32)
            hidden = (hidden.reshape(cells, channels).astype(jnp.float32) + jax.nn.silu(pre_act)).astype(jnp.bfloat16).reshape(hidden.shape)
        delta_y = cotangent[sample]
        for layer_idx in reversed(range(layer_count)):
            patches = taps(stored[layer_idx], frame_count, row_count, col_count, False)
            pre_act = jnp.dot(patches, weights[layer_idx], preferred_element_type=jnp.float32)
            sig_val = jax.nn.sigmoid(pre_act)
            delta_z = (delta_y.reshape(cells, channels).astype(jnp.float32) * sig_val * (1.0 + pre_act * (1.0 - sig_val))).astype(jnp.bfloat16)
            weight_grads[layer_idx] = weight_grads[layer_idx] + lax.dot_general(patches, delta_z, (((0,), (0,)), ((), ())), preferred_element_type=jnp.float32)
            flip_weight = weights[layer_idx].reshape(27, channels, channels).transpose(0, 2, 1).reshape(27 * channels, channels)
            ahead = jnp.pad(delta_z.reshape(delta_y.shape), ((0, 2), (1, 1), (1, 1), (0, 0)))
            adjoint = jnp.dot(taps(ahead, frame_count, row_count, col_count, True), flip_weight, preferred_element_type=jnp.float32)
            delta_y = (delta_y.reshape(cells, channels).astype(jnp.float32) + adjoint).astype(jnp.bfloat16).reshape(delta_y.shape)
    return jnp.stack(weight_grads, 0)
```

```python
import functools

import jax
import jax.numpy as jnp
from jax import lax
from jax.experimental import pallas as pl
from jax.experimental.pallas import tpu as pltpu
from jax.sharding import Mesh
from jax.sharding import PartitionSpec as P

BF16 = jnp.bfloat16
F32 = jnp.float32
CH = 128
COLS = 16
FR = 8
LAYERS = 4
TAPS = 27
KC = TAPS * CH
HALF = KC // 2
PLANE = 9 * CH
OWN = 4
HALO = 7
CHALO = 3
HID = FR * (OWN + 2) * COLS
PART = HID + FR * OWN * COLS


def shifted(x):
    cells = x.shape[0]
    col = lax.broadcasted_iota(jnp.int32, x.shape, 0) % COLS
    before = jnp.where(col == 0, 0.0, pltpu.roll(x, 1, 0))
    after = jnp.where(col == COLS - 1, 0.0, pltpu.roll(x, cells - 1, 0))
    return before.astype(BF16), x.astype(BF16), after.astype(BF16)


def spread(src, im, rows):
    cells = rows * COLS

    @pl.loop(0, FR)
    def _(t):
        for lag_c, v in enumerate(shifted(src[t, : cells + 2 * COLS])):
            for lag_r in range(3):
                at = pl.multiple_of((t + 2) * PLANE + (lag_r * 3 + lag_c) * CH, CH)
                im[:cells, pl.ds(at, CH)] = v[lag_r * COLS : lag_r * COLS + cells]


def inside(first, rows, total):
    row = first + lax.broadcasted_iota(jnp.int32, (rows * COLS, CH), 0) // COLS
    return (row >= 0) & (row < total)


def layers_kernel(
    total, pos, mine, other, w0, r1, r2, r3, q1, q2, q3, o0, o1, o2, o3, wt, wb, im, hid, fac, grad, dz, part
):
    seg, tm, first = pos[0], pos[1], pos[2]
    zero = jnp.zeros((PLANE, CH), BF16)
    for l in range(LAYERS):
        wt[l, KC:, :CH] = zero
        wt[l, :PLANE, CH:] = zero
    wb[KC:, :CH] = zero
    wb[:PLANE, CH:] = zero
    cells = im.shape[0]
    im[:, : 2 * PLANE] = jnp.zeros((cells, 2 * PLANE), BF16)
    im[:, (FR + 2) * PLANE :] = jnp.zeros((cells, 2 * PLANE), BF16)
    own = w0[...]
    wt[seg, :KC, :CH] = own
    wt[seg, PLANE:, CH:] = own
    for d, (r, q) in enumerate(((r1, q1), (r2, q2), (r3, q3)), 1):
        l = lax.rem(seg + LAYERS - d, LAYERS)
        for ref, half in ((r, tm), (q, 1 - tm)):
            at = pl.multiple_of(half * HALF, CH // 2)
            wt[l, pl.ds(at, HALF), :CH] = ref[...]
            wt[l, pl.ds(PLANE + at, HALF), CH:] = ref[...]

    span = OWN + 2 * HALO
    half_fr = FR // 2
    for ref, which in ((mine, tm), (other, 1 - tm)):

        @pl.loop(0, half_fr)
        def _(t):
            rows = ref[t, pl.ds(tm * OWN, span)]
            hid[0, which * half_fr + t, : span * COLS] = rows.reshape(span * COLS, CH).astype(F32)
            at = 2 * HALO + 2 * OWN + tm * OWN
            rows = ref[t, pl.ds(at, OWN + 2 * CHALO)]
            grad[which * half_fr + t] = rows.reshape(-1, CH).astype(F32)

    for l in range(LAYERS):
        rows = span - 2 * (l + 1)
        cells = rows * COLS
        spread(hid.at[l], im, rows)
        keep = slice((6 - 2 * l) * COLS, 10 * COLS)
        kept = (OWN + 2 * l) * COLS

        @pl.loop(0, FR // 2)
        def _(p):
            at = pl.multiple_of(2 * p * PLANE, CH)
            pre2 = jnp.dot(im[:cells, pl.ds(at, 4 * PLANE)], wt[l], preferred_element_type=F32)
            valid = inside(first - HALO + l + 1, rows, total)
            for e in range(2):
                t = 2 * p + e
                pre = pre2[:, e * CH : (e + 1) * CH]
                s = jax.nn.sigmoid(pre)
                if l + 1 < LAYERS:
                    new = hid[l, t, COLS : COLS + cells] + pre * s
                    new = new.astype(BF16).astype(F32)
                    hid[l + 1, t, :cells] = jnp.where(valid, new, 0.0)
                s, pre = s[keep], pre[keep]
                fac[l, t, :kept] = s * (1.0 + pre * (1.0 - s))

    for l in reversed(range(LAYERS)):
        rows = OWN + 2 * l
        cells = rows * COLS
        width = (OWN + 2) * COLS
        own_cells = OWN * COLS

        @pl.loop(0, FR)
        def _(t):
            valid = inside(first - l, rows, total)
            delta = jnp.where(valid, grad[t, :cells] * fac[l, t, :cells], 0.0).astype(BF16)
            at = pl.multiple_of(HID + t * own_cells, own_cells)
            part[l, pl.ds(at, own_cells)] = delta[l * COLS : l * COLS + own_cells]
            at = pl.multiple_of(t * width, width)
            part[l, pl.ds(at, width)] = hid[l, t, (6 - l) * COLS : (6 - l) * COLS + width].astype(
                BF16
            )
            if l > 0:
                dz[t, :cells] = delta.astype(F32)

        if l > 0:
            inner = cells - 2 * COLS
            spread(dz, im, rows - 2)

            @pl.loop(0, TAPS)
            def _(k):
                at = pl.multiple_of((TAPS - 1 - k) * CH, CH)
                block = wt[l, pl.ds(at, CH), :CH].T
                at = pl.multiple_of(k * CH, CH)
                wb[pl.ds(at, CH), :CH] = block
                wb[pl.ds(PLANE + at, CH), CH:] = block

            @pl.loop(0, FR // 2)
            def _(p):
                at = pl.multiple_of((2 * p + 2) * PLANE, CH)
                adjoint = jnp.dot(
                    im[:inner, pl.ds(at, 4 * PLANE)], wb[...], preferred_element_type=F32
                )
                for e in range(2):
                    t = 2 * p + e
                    new = grad[t, COLS : COLS + inner] + adjoint[:, e * CH : (e + 1) * CH]
                    grad[t, :inner] = new.astype(BF16).astype(F32)

    for d, out in enumerate((o0, o1, o2, o3)):
        out[...] = part[lax.rem(seg + d, LAYERS)]


def kernel_grad_kernel(pos, e0, e1, e2, e3, keep, send, x9, d3, wg):
    tm = pos[1]
    cells = OWN * COLS
    width = cells + 2 * COLS
    nothing = jnp.zeros((cells, CH), BF16)
    for m, e in enumerate((e0, e1, e2, e3)):
        for t in range(FR):
            at = (m * FR + t) * cells
            frame = e[t * width : (t + 1) * width].astype(F32)
            for lag_c, v in enumerate(shifted(frame)):
                for lag_r in range(3):
                    tap = (lag_r * 3 + lag_c) * CH
                    x9[at : at + cells, tap : tap + CH] = v[lag_r * COLS : lag_r * COLS + cells]
            for lag_t in range(3):
                src = t + 2 - lag_t
                row = HID + src * cells
                d3[at : at + cells, lag_t * CH : (lag_t + 1) * CH] = (
                    e[row : row + cells] if src < FR else nothing
                )
    out = lax.dot_general(
        d3[...], x9[...], (((0,), (0,)), ((), ())), preferred_element_type=F32
    )
    for lag_t in range(3):
        for tap in range(9):
            at = (lag_t * 9 + tap) * CH
            wg[at : at + CH] = out[lag_t * CH : (lag_t + 1) * CH, tap * CH : (tap + 1) * CH].T
    keep[...] = wg[pl.ds(pl.multiple_of(tm * HALF, CH // 2), HALF)]
    send[...] = wg[pl.ds(pl.multiple_of((1 - tm) * HALF, CH // 2), HALF)].astype(BF16)


def in_vmem(n):
    return [pl.BlockSpec(memory_space=pltpu.SMEM)] + [pl.BlockSpec(memory_space=pltpu.VMEM)] * n


def run_layers(total, pos, *arrays):
    span = OWN + 2 * HALO
    out = jax.ShapeDtypeStruct((PART, CH), BF16)
    return pl.pallas_call(
        functools.partial(layers_kernel, total),
        out_shape=(out,) * LAYERS,
        in_specs=in_vmem(len(arrays)),
        out_specs=(pl.BlockSpec(memory_space=pltpu.VMEM),) * LAYERS,
        scratch_shapes=[
            pltpu.VMEM((LAYERS, 4 * PLANE, 2 * CH), BF16),
            pltpu.VMEM((4 * PLANE, 2 * CH), BF16),
            pltpu.VMEM(((span - 2) * COLS, (FR + 4) * PLANE), BF16),
            pltpu.VMEM((LAYERS, FR, span * COLS, CH), F32),
            pltpu.VMEM((LAYERS, FR, (OWN + 2 * CHALO) * COLS, CH), F32),
            pltpu.VMEM((FR, (OWN + 2 * CHALO) * COLS, CH), F32),
            pltpu.VMEM((FR, (OWN + 2 * CHALO) * COLS, CH), F32),
            pltpu.VMEM((LAYERS, PART, CH), BF16),
        ],
        compiler_params=pltpu.CompilerParams(vmem_limit_bytes=44 * 2**20),
        cost_estimate=pl.CostEstimate(
            flops=9_000_000_000, bytes_accessed=6_000_000, transcendentals=1_000_000
        ),
        name="layers",
    )(pos, *arrays)


def run_kernel_grad(pos, *arrays):
    cells = LAYERS * FR * OWN * COLS
    return pl.pallas_call(
        kernel_grad_kernel,
        out_shape=(
            jax.ShapeDtypeStruct((HALF, CH), F32),
            jax.ShapeDtypeStruct((HALF, CH), BF16),
        ),
        in_specs=in_vmem(len(arrays)),
        out_specs=(pl.BlockSpec(memory_space=pltpu.VMEM),) * 2,
        scratch_shapes=[
            pltpu.VMEM((cells, PLANE), BF16),
            pltpu.VMEM((cells, 3 * CH), BF16),
            pltpu.VMEM((KC, CH), F32),
        ],
        compiler_params=pltpu.CompilerParams(vmem_limit_bytes=32 * 2**20),
        cost_estimate=pl.CostEstimate(
            flops=1_800_000_000, bytes_accessed=4_000_000, transcendentals=0
        ),
        name="kernel_grad",
    )(pos, *arrays)


def ring(count, by):
    return [(i, (i + by) % count) for i in range(count)]


def swap(x):
    return lax.ppermute(x, "tm", [(0, 1), (1, 0)])


def body(inputs, weights, cotangent):
    seg, tm = lax.axis_index("segment"), lax.axis_index("tm")
    space = lax.axis_index(("z", "y"))
    spaces = lax.axis_size(("z", "y"))
    ny, nz = lax.axis_size("y"), lax.axis_size("z")
    rows = inputs.shape[2]
    pos = jnp.stack([seg, tm, space * rows + tm * OWN]).astype(jnp.int32)

    w = weights[0]
    half = lax.dynamic_slice_in_dim(w, tm * HALF, HALF, 0)
    got = [lax.ppermute(half, "segment", ring(LAYERS, d)) for d in (1, 2, 3)]
    crossed = [swap(g) for g in got]

    x = lax.dynamic_index_in_dim(inputs, seg, 0, keepdims=False)
    c = lax.dynamic_index_in_dim(cotangent, seg, 0, keepdims=False)
    down = [(i, i + 1) for i in range(spaces - 1)]
    up = [(i + 1, i) for i in range(spaces - 1)]
    before = lax.ppermute(
        jnp.concatenate([x[:, rows - HALO :], c[:, rows - CHALO :]], 1), ("z", "y"), down
    )
    after = lax.ppermute(jnp.concatenate([x[:, :HALO], c[:, :CHALO]], 1), ("z", "y"), up)
    mine = jnp.concatenate(
        [before[:, :HALO], x, after[:, :HALO], before[:, HALO:], c, after[:, HALO:]], 1
    )
    other = swap(mine)

    parts = run_layers(spaces * rows, pos, mine, other, w, *got, *crossed)
    moved = [lax.ppermute(parts[d], "segment", ring(LAYERS, d)) for d in (1, 2, 3)]
    keep, send = run_kernel_grad(pos, parts[0], *moved)

    total = (keep + swap(send).astype(F32)).astype(BF16)
    rows_y = HALF // ny
    pieces = lax.all_to_all(total.reshape(ny, rows_y, CH), "y", 0, 0)
    total = jnp.sum(pieces.astype(F32), 0).astype(BF16)
    rows_z = -(-rows_y // (16 * nz)) * 16
    total = jnp.pad(total, ((0, nz * rows_z - rows_y), (0, 0)))
    pieces = lax.all_to_all(total.reshape(nz, rows_z, CH), "z", 0, 0)
    total = jnp.sum(pieces.astype(F32), 0).astype(BF16)
    whole = lax.all_to_all(jnp.broadcast_to(total, (nz, rows_z, CH)), "z", 0, 0)
    whole = whole.reshape(nz * rows_z, CH)[:rows_y]
    whole = lax.all_to_all(jnp.broadcast_to(whole, (ny, rows_y, CH)), "y", 0, 0)
    whole = whole.reshape(HALF, CH)
    theirs = swap(whole)
    low = jnp.where(tm == 0, whole, theirs)
    high = jnp.where(tm == 0, theirs, whole)
    return jnp.concatenate([low, high], 0).astype(F32)[None]


def solution(mesh):
    segments, cores, spaces = mesh.devices.shape
    ny = 4 if spaces % 4 == 0 else 1
    fine = Mesh(
        mesh.devices.reshape(segments, cores, spaces // ny, ny), ("segment", "tm", "z", "y")
    )
    spec = P(None, "tm", ("z", "y"), None, None)
    return jax.shard_map(
        body,
        mesh=fine,
        in_specs=(spec, P("segment", None, None), spec),
        out_specs=P("segment", None, None),
        check_vma=False,
    )
```

```python
import functools

import jax
import jax.numpy as jnp
from jax import lax
from jax.experimental import pallas as pl
from jax.experimental.pallas import tpu as pltpu
from jax.sharding import Mesh
from jax.sharding import PartitionSpec as P

BF16 = jnp.bfloat16
F32 = jnp.float32
CH = 128
COLS = 16
FR = 8
LAYERS = 4
TAPS = 27
KC = TAPS * CH
HALF = KC // 2
PLANE = 9 * CH
OWN = 4
HALO = 7
CHALO = 3
HID = FR * (OWN + 2) * COLS
PART = HID + FR * OWN * COLS


def shifted(x):
    cells = x.shape[0]
    col = lax.broadcasted_iota(jnp.int32, x.shape, 0) % COLS
    before = jnp.where(col == 0, 0.0, pltpu.roll(x, 1, 0))
    after = jnp.where(col == COLS - 1, 0.0, pltpu.roll(x, cells - 1, 0))
    return before.astype(BF16), x.astype(BF16), after.astype(BF16)


def inside(first, rows, total):
    row = first + lax.broadcasted_iota(jnp.int32, (rows * COLS, CH), 0) // COLS
    return (row >= 0) & (row < total)


def taps_of(cols, frames, cells):
    return jnp.concatenate(
        [
            cols[t * 3 + lag_c, lag_r * COLS : lag_r * COLS + cells]
            for t in frames
            for lag_r in range(3)
            for lag_c in range(3)
        ],
        1,
    )


def pair_kernel(ref, base, first):
    rows = (4 - first) * PLANE
    at = base + first * PLANE
    return jnp.concatenate(
        [ref[pl.ds(at + PLANE, rows)], ref[pl.ds(at, rows)]],
        1,
    )


def layers_kernel(
    total, pos, mine, other, w0, r1, r2, r3, q1, q2, q3, o0, o1, o2, o3, wz, wb, cols, fac, grad, part
):
    seg, tm, first = pos[0], pos[1], pos[2]
    step = PLANE + KC
    zero = jnp.zeros((PLANE, CH), BF16)
    for l in range(LAYERS + 1):
        wz[l * step : l * step + PLANE] = zero
    for l in range(LAYERS):
        wb[l * step : l * step + PLANE] = zero
    wz[pl.ds(pl.multiple_of(seg * step + PLANE, CH), KC)] = w0[...]
    for d, (r, q) in enumerate(((r1, q1), (r2, q2), (r3, q3)), 1):
        at = lax.rem(seg + LAYERS - d, LAYERS) * step + PLANE
        wz[pl.ds(pl.multiple_of(at + tm * HALF, CH // 2), HALF)] = r[...]
        wz[pl.ds(pl.multiple_of(at + (1 - tm) * HALF, CH // 2), HALF)] = q[...]

    span = OWN + 2 * HALO
    half_fr = FR // 2
    for ref, which in ((mine, tm), (other, 1 - tm)):

        @pl.loop(0, half_fr)
        def _(t):
            frame = which * half_fr + t
            rows = ref[t, pl.ds(tm * OWN, span)]
            for lag_c, v in enumerate(shifted(rows.reshape(span * COLS, CH).astype(F32))):
                cols[0, frame * 3 + lag_c] = v
            at = 2 * HALO + 2 * OWN + tm * OWN
            rows = ref[t, pl.ds(at, OWN + 2 * CHALO)]
            grad[frame] = rows.reshape(-1, CH).astype(F32)

    width = (OWN + 2) * COLS
    own_cells = OWN * COLS

    def set_delta(l, t, value, to):
        cells = value.shape[0]
        valid = inside(first - l, OWN + 2 * l, total)
        delta = jnp.where(valid, value, 0.0).astype(BF16)
        at = HID + t * own_cells
        part[l, at : at + own_cells] = delta[l * COLS : l * COLS + own_cells]
        if l > 0:
            for lag_c, v in enumerate(shifted(delta.astype(F32))):
                to[t * 3 + lag_c, :cells] = v

    for l in range(LAYERS):
        rows = span - 2 * (l + 1)
        cells = rows * COLS
        src, dst = cols.at[l % 2], cols.at[(l + 1) % 2]
        for t in range(FR):
            at = (6 - l) * COLS
            part[l, t * width : (t + 1) * width] = src[t * 3 + 1, at : at + width]
        if l > 0:
            for k in range(TAPS):
                at = l * step + PLANE + (TAPS - 1 - k) * CH
                to = (l - 1) * step + PLANE + k * CH
                wb[to : to + CH] = wz[at : at + CH].T
        keep = slice((6 - 2 * l) * COLS, 10 * COLS)
        kept = (OWN + 2 * l) * COLS
        valid = inside(first - HALO + l + 1, rows, total)
        for p in range(FR // 2):
            lo = max(0, 2 * p - 2)
            pre2 = jnp.dot(
                taps_of(src, range(lo, 2 * p + 2), cells),
                pair_kernel(wz, l * step, 0 if p else 2),
                preferred_element_type=F32,
            )
            for e in range(2):
                t = 2 * p + e
                pre = pre2[:, e * CH : (e + 1) * CH]
                s = jax.nn.sigmoid(pre)
                if l + 1 < LAYERS:
                    new = src[t * 3 + 1, COLS : COLS + cells].astype(F32) + pre * s
                    new = jnp.where(valid, new, 0.0).astype(BF16).astype(F32)
                    for lag_c, v in enumerate(shifted(new)):
                        dst[t * 3 + lag_c, :cells] = v
                s, pre = s[keep], pre[keep]
                slope = s * (1.0 + pre * (1.0 - s))
                if l + 1 < LAYERS:
                    fac[l, t, :kept] = slope
                else:
                    set_delta(l, t, grad[t] * slope, dst)

    for l in reversed(range(1, LAYERS)):
        cells = (OWN + 2 * (l - 1)) * COLS
        src, dst = cols.at[(l + 1) % 2], cols.at[l % 2]
        for pairs in ((0, 1, 2), (3,)):
            hi = 4 if len(pairs) > 1 else 2
            lhs = [taps_of(src, range(2 * p, 2 * p + hi), cells) for p in pairs]
            kernel = pair_kernel(wb, (l - 1) * step, 0)[: hi * PLANE]
            adjoint = jnp.dot(jnp.concatenate(lhs, 0), kernel, preferred_element_type=F32)
            for i, p in enumerate(pairs):
                for e in range(2):
                    t = 2 * p + e
                    mine_of = adjoint[i * cells : (i + 1) * cells, e * CH : (e + 1) * CH]
                    new = grad[t, COLS : COLS + cells] + mine_of
                    new = new.astype(BF16).astype(F32)
                    if l > 1:
                        grad[t, :cells] = new
                    set_delta(l - 1, t, new * fac[l - 1, t, :cells], dst)

    for d, out in enumerate((o0, o1, o2, o3)):
        out[...] = part[lax.rem(seg + d, LAYERS)]


def kernel_grad_kernel(pos, e0, e1, e2, e3, keep, send, x9, d3, wg):
    tm = pos[1]
    cells = OWN * COLS
    width = cells + 2 * COLS
    nothing = jnp.zeros((cells, CH), BF16)
    for m, e in enumerate((e0, e1, e2, e3)):
        for t in range(FR):
            at = (m * FR + t) * cells
            frame = e[t * width : (t + 1) * width].astype(F32)
            for lag_c, v in enumerate(shifted(frame)):
                for lag_r in range(3):
                    tap = (lag_r * 3 + lag_c) * CH
                    x9[at : at + cells, tap : tap + CH] = v[lag_r * COLS : lag_r * COLS + cells]
            for lag_t in range(3):
                src = t + 2 - lag_t
                row = HID + src * cells
                d3[at : at + cells, lag_t * CH : (lag_t + 1) * CH] = (
                    e[row : row + cells] if src < FR else nothing
                )
    out = lax.dot_general(
        d3[...], x9[...], (((0,), (0,)), ((), ())), preferred_element_type=F32
    )
    for lag_t in range(3):
        for tap in range(9):
            at = (lag_t * 9 + tap) * CH
            wg[at : at + CH] = out[lag_t * CH : (lag_t + 1) * CH, tap * CH : (tap + 1) * CH].T
    keep[...] = wg[pl.ds(pl.multiple_of(tm * HALF, CH // 2), HALF)]
    send[...] = wg[pl.ds(pl.multiple_of((1 - tm) * HALF, CH // 2), HALF)].astype(BF16)


def in_vmem(n):
    return [pl.BlockSpec(memory_space=pltpu.SMEM)] + [pl.BlockSpec(memory_space=pltpu.VMEM)] * n


def run_layers(total, pos, *arrays):
    span = OWN + 2 * HALO
    out = jax.ShapeDtypeStruct((PART, CH), BF16)
    return pl.pallas_call(
        functools.partial(layers_kernel, total),
        out_shape=(out,) * LAYERS,
        in_specs=in_vmem(len(arrays)),
        out_specs=(pl.BlockSpec(memory_space=pltpu.VMEM),) * LAYERS,
        scratch_shapes=[
            pltpu.VMEM((PLANE + LAYERS * (PLANE + KC), CH), BF16),
            pltpu.VMEM((PLANE + (LAYERS - 1) * (PLANE + KC), CH), BF16),
            pltpu.VMEM((2, FR * 3, span * COLS, CH), BF16),
            pltpu.VMEM((LAYERS - 1, FR, (OWN + 2 * CHALO) * COLS, CH), F32),
            pltpu.VMEM((FR, (OWN + 2 * CHALO) * COLS, CH), F32),
            pltpu.VMEM((LAYERS, PART, CH), BF16),
        ],
        compiler_params=pltpu.CompilerParams(vmem_limit_bytes=44 * 2**20),
        cost_estimate=pl.CostEstimate(
            flops=9_000_000_000, bytes_accessed=6_000_000, transcendentals=1_000_000
        ),
        name="layers",
    )(pos, *arrays)


def run_kernel_grad(pos, *arrays):
    cells = LAYERS * FR * OWN * COLS
    return pl.pallas_call(
        kernel_grad_kernel,
        out_shape=(
            jax.ShapeDtypeStruct((HALF, CH), F32),
            jax.ShapeDtypeStruct((HALF, CH), BF16),
        ),
        in_specs=in_vmem(len(arrays)),
        out_specs=(pl.BlockSpec(memory_space=pltpu.VMEM),) * 2,
        scratch_shapes=[
            pltpu.VMEM((cells, PLANE), BF16),
            pltpu.VMEM((cells, 3 * CH), BF16),
            pltpu.VMEM((KC, CH), F32),
        ],
        compiler_params=pltpu.CompilerParams(vmem_limit_bytes=32 * 2**20),
        cost_estimate=pl.CostEstimate(
            flops=1_800_000_000, bytes_accessed=4_000_000, transcendentals=0
        ),
        name="kernel_grad",
    )(pos, *arrays)


def ring(count, by):
    return [(i, (i + by) % count) for i in range(count)]


def swap(x):
    return lax.ppermute(x, "tm", [(0, 1), (1, 0)])


def body(inputs, weights, cotangent):
    seg, tm = lax.axis_index("segment"), lax.axis_index("tm")
    space = lax.axis_index(("z", "y"))
    spaces = lax.axis_size(("z", "y"))
    ny, nz = lax.axis_size("y"), lax.axis_size("z")
    rows = inputs.shape[2]
    pos = jnp.stack([seg, tm, space * rows + tm * OWN]).astype(jnp.int32)

    w = weights[0]
    half = lax.dynamic_slice_in_dim(w, tm * HALF, HALF, 0)
    got = [lax.ppermute(half, "segment", ring(LAYERS, d)) for d in (1, 2, 3)]
    crossed = [swap(g) for g in got]

    x = lax.dynamic_index_in_dim(inputs, seg, 0, keepdims=False)
    c = lax.dynamic_index_in_dim(cotangent, seg, 0, keepdims=False)
    down = [(i, i + 1) for i in range(spaces - 1)]
    up = [(i + 1, i) for i in range(spaces - 1)]
    before = lax.ppermute(
        jnp.concatenate([x[:, rows - HALO :], c[:, rows - CHALO :]], 1), ("z", "y"), down
    )
    after = lax.ppermute(jnp.concatenate([x[:, :HALO], c[:, :CHALO]], 1), ("z", "y"), up)
    mine = jnp.concatenate(
        [before[:, :HALO], x, after[:, :HALO], before[:, HALO:], c, after[:, HALO:]], 1
    )
    other = swap(mine)

    parts = run_layers(spaces * rows, pos, mine, other, w, *got, *crossed)
    moved = [lax.ppermute(parts[d], "segment", ring(LAYERS, d)) for d in (1, 2, 3)]
    keep, send = run_kernel_grad(pos, parts[0], *moved)

    total = (keep + swap(send).astype(F32)).astype(BF16)
    rows_y = HALF // ny
    pieces = lax.all_to_all(total.reshape(ny, rows_y, CH), "y", 0, 0)
    total = jnp.sum(pieces.astype(F32), 0).astype(BF16)
    rows_z = -(-rows_y // (16 * nz)) * 16
    total = jnp.pad(total, ((0, nz * rows_z - rows_y), (0, 0)))
    pieces = lax.all_to_all(total.reshape(nz, rows_z, CH), "z", 0, 0)
    total = jnp.sum(pieces.astype(F32), 0).astype(BF16)
    whole = lax.all_to_all(jnp.broadcast_to(total, (nz, rows_z, CH)), "z", 0, 0)
    whole = whole.reshape(nz * rows_z, CH)[:rows_y]
    whole = lax.all_to_all(jnp.broadcast_to(whole, (ny, rows_y, CH)), "y", 0, 0)
    whole = whole.reshape(HALF, CH)
    theirs = swap(whole)
    low = jnp.where(tm == 0, whole, theirs)
    high = jnp.where(tm == 0, theirs, whole)
    return jnp.concatenate([low, high], 0).astype(F32)[None]


def solution(mesh):
    segments, cores, spaces = mesh.devices.shape
    ny = 4 if spaces % 4 == 0 else 1
    fine = Mesh(
        mesh.devices.reshape(segments, cores, spaces // ny, ny), ("segment", "tm", "z", "y")
    )
    spec = P(None, "tm", ("z", "y"), None, None)
    return jax.shard_map(
        body,
        mesh=fine,
        in_specs=(spec, P("segment", None, None), spec),
        out_specs=P("segment", None, None),
        check_vma=False,
    )
```

```python
import functools

import jax
import jax.numpy as jnp
from jax import lax
from jax.experimental import pallas as pl
from jax.experimental.pallas import tpu as pltpu
from jax.sharding import Mesh
from jax.sharding import PartitionSpec as P

BF16 = jnp.bfloat16
F32 = jnp.float32
CH = 128
COLS = 16
FR = 8
LAYERS = 4
TAPS = 27
KC = TAPS * CH
HALF = KC // 2
PLANE = 9 * CH
OWN = 4
HALO = 7
CHALO = 3
HID = FR * (OWN + 2) * COLS
PART = HID + FR * OWN * COLS


def shifted(x):
    cells = x.shape[0]
    col = lax.broadcasted_iota(jnp.int32, x.shape, 0) % COLS
    before = jnp.where(col == 0, 0.0, pltpu.roll(x, 1, 0))
    after = jnp.where(col == COLS - 1, 0.0, pltpu.roll(x, cells - 1, 0))
    return before.astype(BF16), x.astype(BF16), after.astype(BF16)


def inside(first, rows, total):
    row = first + lax.broadcasted_iota(jnp.int32, (rows * COLS, CH), 0) // COLS
    return (row >= 0) & (row < total)


def taps_of(cols, frames, cells):
    return jnp.concatenate(
        [
            cols[t * 3 + lag_c, lag_r * COLS : lag_r * COLS + cells]
            for t in frames
            for lag_r in range(3)
            for lag_c in range(3)
        ],
        1,
    )


def pair_kernel(ref, base, first):
    rows = (4 - first) * PLANE
    at = base + first * PLANE
    return jnp.concatenate(
        [ref[pl.ds(at + PLANE, rows)], ref[pl.ds(at, rows)]],
        1,
    )


def layers_kernel(
    total, pos, mine, other, w0, r1, r3, ra, rb, q1, q3, qa, qb, *rest
):
    o0, o1, oa, ob, o3, wz, wb, cols, fac, grad, part = rest
    seg, tm, first = pos[0], pos[1], pos[2]
    step = PLANE + KC
    zero = jnp.zeros((PLANE, CH), BF16)
    for l in range(LAYERS + 1):
        wz[l * step : l * step + PLANE] = zero
    for l in range(LAYERS):
        wb[l * step : l * step + PLANE] = zero
    wz[pl.ds(pl.multiple_of(seg * step + PLANE, CH), KC)] = w0[...]
    for d, skip, r, q in ((1, 0, r1, q1), (3, 0, r3, q3), (2, 0, ra, qa), (2, HALF // 2, rb, qb)):
        at = lax.rem(seg + LAYERS - d, LAYERS) * step + PLANE + skip
        for ref, half in ((r, tm), (q, 1 - tm)):
            wz[pl.ds(pl.multiple_of(at + half * HALF, 32), ref.shape[0])] = ref[...]

    span = OWN + 2 * HALO
    half_fr = FR // 2
    for ref, which in ((mine, tm), (other, 1 - tm)):

        @pl.loop(0, half_fr)
        def _(t):
            frame = which * half_fr + t
            rows = ref[t, pl.ds(tm * OWN, span)]
            for lag_c, v in enumerate(shifted(rows.reshape(span * COLS, CH).astype(F32))):
                cols[0, frame * 3 + lag_c] = v
            at = 2 * HALO + 2 * OWN + tm * OWN
            rows = ref[t, pl.ds(at, OWN + 2 * CHALO)]
            grad[frame] = rows.reshape(-1, CH).astype(F32)

    width = (OWN + 2) * COLS
    own_cells = OWN * COLS

    def set_delta(l, t, value, to):
        cells = value.shape[0]
        valid = inside(first - l, OWN + 2 * l, total)
        delta = jnp.where(valid, value, 0.0).astype(BF16)
        at = HID + t * own_cells
        part[l, at : at + own_cells] = delta[l * COLS : l * COLS + own_cells]
        if l > 0:
            for lag_c, v in enumerate(shifted(delta.astype(F32))):
                to[t * 3 + lag_c, :cells] = v

    for l in range(LAYERS):
        rows = span - 2 * (l + 1)
        cells = rows * COLS
        src, dst = cols.at[l % 2], cols.at[(l + 1) % 2]
        for t in range(FR):
            at = (6 - l) * COLS
            part[l, t * width : (t + 1) * width] = src[t * 3 + 1, at : at + width]
        if l > 0:
            for k in range(TAPS):
                at = l * step + PLANE + (TAPS - 1 - k) * CH
                to = (l - 1) * step + PLANE + k * CH
                wb[to : to + CH] = wz[at : at + CH].T
        keep = slice((6 - 2 * l) * COLS, 10 * COLS)
        kept = (OWN + 2 * l) * COLS
        valid = inside(first - HALO + l + 1, rows, total)
        for p in range(FR // 2):
            lo = max(0, 2 * p - 2)
            pre2 = jnp.dot(
                taps_of(src, range(lo, 2 * p + 2), cells),
                pair_kernel(wz, l * step, 0 if p else 2),
                preferred_element_type=F32,
            )
            for e in range(2):
                t = 2 * p + e
                pre = pre2[:, e * CH : (e + 1) * CH]
                s = jax.nn.sigmoid(pre)
                if l + 1 < LAYERS:
                    new = src[t * 3 + 1, COLS : COLS + cells].astype(F32) + pre * s
                    new = jnp.where(valid, new, 0.0).astype(BF16).astype(F32)
                    for lag_c, v in enumerate(shifted(new)):
                        dst[t * 3 + lag_c, :cells] = v
                s, pre = s[keep], pre[keep]
                slope = s * (1.0 + pre * (1.0 - s))
                if l + 1 < LAYERS:
                    fac[l, t, :kept] = slope
                else:
                    set_delta(l, t, grad[t] * slope, dst)

    for l in reversed(range(1, LAYERS)):
        cells = (OWN + 2 * (l - 1)) * COLS
        src, dst = cols.at[(l + 1) % 2], cols.at[l % 2]
        for pairs in ((0, 1, 2), (3,)):
            hi = 4 if len(pairs) > 1 else 2
            lhs = [taps_of(src, range(2 * p, 2 * p + hi), cells) for p in pairs]
            kernel = pair_kernel(wb, (l - 1) * step, 0)[: hi * PLANE]
            adjoint = jnp.dot(jnp.concatenate(lhs, 0), kernel, preferred_element_type=F32)
            for i, p in enumerate(pairs):
                for e in range(2):
                    t = 2 * p + e
                    mine_of = adjoint[i * cells : (i + 1) * cells, e * CH : (e + 1) * CH]
                    new = grad[t, COLS : COLS + cells] + mine_of
                    new = new.astype(BF16).astype(F32)
                    if l > 1:
                        grad[t, :cells] = new
                    set_delta(l - 1, t, new * fac[l - 1, t, :cells], dst)

    for d, lo, out in ((0, 0, o0), (1, 0, o1), (2, 0, oa), (2, PART // 2, ob), (3, 0, o3)):
        out[...] = part[lax.rem(seg + d, LAYERS), lo : lo + out.shape[0]]


def kernel_grad_kernel(pos, e0, e1, e3, ea, eb, keep, send, e2, x9, d3, wg):
    tm = pos[1]
    e2[: PART // 2] = ea[...]
    e2[PART // 2 :] = eb[...]
    cells = OWN * COLS
    width = cells + 2 * COLS
    nothing = jnp.zeros((cells, CH), BF16)
    for m, e in enumerate((e0, e1, e2, e3)):
        for t in range(FR):
            at = (m * FR + t) * cells
            frame = e[t * width : (t + 1) * width].astype(F32)
            for lag_c, v in enumerate(shifted(frame)):
                for lag_r in range(3):
                    tap = (lag_r * 3 + lag_c) * CH
                    x9[at : at + cells, tap : tap + CH] = v[lag_r * COLS : lag_r * COLS + cells]
            for lag_t in range(3):
                src = t + 2 - lag_t
                row = HID + src * cells
                d3[at : at + cells, lag_t * CH : (lag_t + 1) * CH] = (
                    e[row : row + cells] if src < FR else nothing
                )
    out = lax.dot_general(
        d3[...], x9[...], (((0,), (0,)), ((), ())), preferred_element_type=F32
    )
    for lag_t in range(3):
        for tap in range(9):
            at = (lag_t * 9 + tap) * CH
            wg[at : at + CH] = out[lag_t * CH : (lag_t + 1) * CH, tap * CH : (tap + 1) * CH].T
    keep[...] = wg[pl.ds(pl.multiple_of(tm * HALF, CH // 2), HALF)]
    send[...] = wg[pl.ds(pl.multiple_of((1 - tm) * HALF, CH // 2), HALF)].astype(BF16)


def in_vmem(n):
    return [pl.BlockSpec(memory_space=pltpu.SMEM)] + [pl.BlockSpec(memory_space=pltpu.VMEM)] * n


def run_layers(total, pos, *arrays):
    span = OWN + 2 * HALO
    lengths = (PART, PART, PART // 2, PART // 2, PART)
    return pl.pallas_call(
        functools.partial(layers_kernel, total),
        out_shape=tuple(jax.ShapeDtypeStruct((n, CH), BF16) for n in lengths),
        in_specs=in_vmem(len(arrays)),
        out_specs=(pl.BlockSpec(memory_space=pltpu.VMEM),) * len(lengths),
        scratch_shapes=[
            pltpu.VMEM((PLANE + LAYERS * (PLANE + KC), CH), BF16),
            pltpu.VMEM((PLANE + (LAYERS - 1) * (PLANE + KC), CH), BF16),
            pltpu.VMEM((2, FR * 3, span * COLS, CH), BF16),
            pltpu.VMEM((LAYERS - 1, FR, (OWN + 2 * CHALO) * COLS, CH), F32),
            pltpu.VMEM((FR, (OWN + 2 * CHALO) * COLS, CH), F32),
            pltpu.VMEM((LAYERS, PART, CH), BF16),
        ],
        compiler_params=pltpu.CompilerParams(vmem_limit_bytes=44 * 2**20),
        cost_estimate=pl.CostEstimate(
            flops=9_000_000_000, bytes_accessed=6_000_000, transcendentals=1_000_000
        ),
        name="layers",
    )(pos, *arrays)


def run_kernel_grad(pos, *arrays):
    cells = LAYERS * FR * OWN * COLS
    return pl.pallas_call(
        kernel_grad_kernel,
        out_shape=(
            jax.ShapeDtypeStruct((HALF, CH), F32),
            jax.ShapeDtypeStruct((HALF, CH), BF16),
        ),
        in_specs=in_vmem(len(arrays)),
        out_specs=(pl.BlockSpec(memory_space=pltpu.VMEM),) * 2,
        scratch_shapes=[
            pltpu.VMEM((PART, CH), BF16),
            pltpu.VMEM((cells, PLANE), BF16),
            pltpu.VMEM((cells, 3 * CH), BF16),
            pltpu.VMEM((KC, CH), F32),
        ],
        compiler_params=pltpu.CompilerParams(vmem_limit_bytes=32 * 2**20),
        cost_estimate=pl.CostEstimate(
            flops=1_800_000_000, bytes_accessed=4_000_000, transcendentals=0
        ),
        name="kernel_grad",
    )(pos, *arrays)


def ring(count, by):
    return [(i, (i + by) % count) for i in range(count)]


def along(x, by):
    return lax.ppermute(x, "segment", ring(LAYERS, by))


def swap(x):
    return lax.ppermute(x, "tm", [(0, 1), (1, 0)])


def body(inputs, weights, cotangent):
    seg, tm = lax.axis_index("segment"), lax.axis_index("tm")
    space = lax.axis_index(("z", "y"))
    spaces = lax.axis_size(("z", "y"))
    ny, nz = lax.axis_size("y"), lax.axis_size("z")
    rows = inputs.shape[2]
    pos = jnp.stack([seg, tm, space * rows + tm * OWN]).astype(jnp.int32)

    w = weights[0]
    half = lax.dynamic_slice_in_dim(w, tm * HALF, HALF, 0)
    left, right = along(half, 1), along(half, -1)
    got = [left, right, along(left[: HALF // 2], 1), along(right[HALF // 2 :], -1)]
    crossed = [swap(g) for g in got]

    x = lax.dynamic_index_in_dim(inputs, seg, 0, keepdims=False)
    c = lax.dynamic_index_in_dim(cotangent, seg, 0, keepdims=False)
    down = [(i, i + 1) for i in range(spaces - 1)]
    up = [(i + 1, i) for i in range(spaces - 1)]
    before = lax.ppermute(
        jnp.concatenate([x[:, rows - HALO :], c[:, rows - CHALO :]], 1), ("z", "y"), down
    )
    after = lax.ppermute(jnp.concatenate([x[:, :HALO], c[:, :CHALO]], 1), ("z", "y"), up)
    mine = jnp.concatenate(
        [before[:, :HALO], x, after[:, :HALO], before[:, HALO:], c, after[:, HALO:]], 1
    )
    other = swap(mine)

    parts = run_layers(spaces * rows, pos, mine, other, w, *got, *crossed)
    far_a, far_b = along(parts[2], 1), along(parts[3], -1)
    near = [along(parts[1], 1), along(parts[4], -1)]
    keep, send = run_kernel_grad(pos, parts[0], *near, along(far_a, 1), along(far_b, -1))

    total = (keep + swap(send).astype(F32)).astype(BF16)
    rows_y = HALF // ny
    pieces = lax.all_to_all(total.reshape(ny, rows_y, CH), "y", 0, 0)
    total = jnp.sum(pieces.astype(F32), 0).astype(BF16)
    rows_z = -(-rows_y // (16 * nz)) * 16
    total = jnp.pad(total, ((0, nz * rows_z - rows_y), (0, 0)))
    pieces = lax.all_to_all(total.reshape(nz, rows_z, CH), "z", 0, 0)
    total = jnp.sum(pieces.astype(F32), 0).astype(BF16)
    whole = lax.all_to_all(jnp.broadcast_to(total, (nz, rows_z, CH)), "z", 0, 0)
    whole = whole.reshape(nz * rows_z, CH)[:rows_y]
    whole = lax.all_to_all(jnp.broadcast_to(whole, (ny, rows_y, CH)), "y", 0, 0)
    whole = whole.reshape(HALF, CH)
    theirs = swap(whole)
    low = jnp.where(tm == 0, whole, theirs)
    high = jnp.where(tm == 0, theirs, whole)
    return jnp.concatenate([low, high], 0).astype(F32)[None]


def solution(mesh):
    segments, cores, spaces = mesh.devices.shape
    ny = 4 if spaces % 4 == 0 else 1
    fine = Mesh(
        mesh.devices.reshape(segments, cores, spaces // ny, ny), ("segment", "tm", "z", "y")
    )
    spec = P(None, "tm", ("z", "y"), None, None)
    return jax.shard_map(
        body,
        mesh=fine,
        in_specs=(spec, P("segment", None, None), spec),
        out_specs=P("segment", None, None),
        check_vma=False,
    )
```

```python
import functools

import jax
import jax.numpy as jnp
from jax import lax
from jax.experimental import pallas as pl
from jax.experimental.pallas import tpu as pltpu
from jax.sharding import Mesh
from jax.sharding import PartitionSpec as P

BF16 = jnp.bfloat16
F32 = jnp.float32
CH = 128
COLS = 16
FR = 8
LAYERS = 4
TAPS = 27
KC = TAPS * CH
HALF = KC // 2
PLANE = 9 * CH
OWN = 4
HALO = 7
CHALO = 3
HID = FR * (OWN + 2) * COLS
PART = HID + FR * OWN * COLS


def shifted(x):
    cells = x.shape[0]
    col = lax.broadcasted_iota(jnp.int32, x.shape, 0) % COLS
    before = jnp.where(col == 0, 0.0, pltpu.roll(x, 1, 0))
    after = jnp.where(col == COLS - 1, 0.0, pltpu.roll(x, cells - 1, 0))
    return before.astype(BF16), x.astype(BF16), after.astype(BF16)


def inside(first, rows, total):
    row = first + lax.broadcasted_iota(jnp.int32, (rows * COLS, CH), 0) // COLS
    return (row >= 0) & (row < total)


def taps_of(cols, frames, cells):
    return jnp.concatenate(
        [
            cols[t * 3 + lag_c, lag_r * COLS : lag_r * COLS + cells]
            for t in frames
            for lag_r in range(3)
            for lag_c in range(3)
        ],
        1,
    )


def pair_kernel(ref, base, first):
    rows = (4 - first) * PLANE
    at = base + first * PLANE
    return jnp.concatenate(
        [ref[pl.ds(at + PLANE, rows)], ref[pl.ds(at, rows)]],
        1,
    )


def layers_kernel(
    total, pos, mine, other, long, short, w0, r1, r3, ra, rb, q1, q3, qa, qb, *rest
):
    o0, o1, oa, ob, o3, wz, wb, cols, fac, grad, part = rest
    seg, tm, first = pos[0], pos[1], pos[2]
    step = PLANE + KC
    zero = jnp.zeros((PLANE, CH), BF16)
    for l in range(LAYERS + 1):
        wz[l * step : l * step + PLANE] = zero
    for l in range(LAYERS):
        wb[l * step : l * step + PLANE] = zero
    wz[pl.ds(pl.multiple_of(seg * step + PLANE, CH), KC)] = w0[...]
    for d, skip, r, q in ((1, 0, r1, q1), (3, 0, r3, q3), (2, 0, ra, qa), (2, HALF // 2, rb, qb)):
        at = lax.rem(seg + LAYERS - d, LAYERS) * step + PLANE + skip
        for ref, half in ((r, tm), (q, 1 - tm)):
            wz[pl.ds(pl.multiple_of(at + half * HALF, 32), ref.shape[0])] = ref[...]

    span = OWN + 2 * HALO
    half_fr = FR // 2
    band = 2 * OWN
    near = HALO - OWN
    upper = 1 - tm

    def put(t, to, rows):
        cells = rows.shape[0] * COLS
        at = pl.multiple_of(to * COLS, COLS)
        cols[0, t * 3 + 1, pl.ds(at, cells)] = rows.reshape(cells, CH)

    def put_grad(t, to, rows):
        cells = rows.shape[0] * COLS
        at = pl.multiple_of(to * COLS, COLS)
        grad[t, pl.ds(at, cells)] = rows.reshape(cells, CH).astype(F32)

    for i, (ref, which) in enumerate(((mine, tm), (other, upper))):

        @pl.loop(0, half_fr)
        def _(t):
            frame = which * half_fr + t
            side = i * half_fr + t
            put(frame, tm * (near + band), long[side, :HALO])
            put(frame, near + upper * OWN, ref[t, :band])
            put(frame, upper * (HALO + band), short[side])
            for lag_c, v in enumerate(shifted(cols[0, frame * 3 + 1].astype(F32))):
                if lag_c != 1:
                    cols[0, frame * 3 + lag_c] = v
            rest_rows = band - 1
            put_grad(frame, upper * CHALO, ref[t, pl.ds(band + tm, rest_rows)])
            put_grad(frame, tm * rest_rows, long[side, HALO:])

    width = (OWN + 2) * COLS
    own_cells = OWN * COLS

    def set_delta(l, t, value, to):
        cells = value.shape[0]
        valid = inside(first - l, OWN + 2 * l, total)
        delta = jnp.where(valid, value, 0.0).astype(BF16)
        at = HID + t * own_cells
        part[l, at : at + own_cells] = delta[l * COLS : l * COLS + own_cells]
        if l > 0:
            for lag_c, v in enumerate(shifted(delta.astype(F32))):
                to[t * 3 + lag_c, :cells] = v

    for l in range(LAYERS):
        rows = span - 2 * (l + 1)
        cells = rows * COLS
        src, dst = cols.at[l % 2], cols.at[(l + 1) % 2]
        for t in range(FR):
            at = (6 - l) * COLS
            part[l, t * width : (t + 1) * width] = src[t * 3 + 1, at : at + width]
        if l > 0:
            for k in range(TAPS):
                at = l * step + PLANE + (TAPS - 1 - k) * CH
                to = (l - 1) * step + PLANE + k * CH
                wb[to : to + CH] = wz[at : at + CH].T
        keep = slice((6 - 2 * l) * COLS, 10 * COLS)
        kept = (OWN + 2 * l) * COLS
        valid = inside(first - HALO + l + 1, rows, total)
        for p in range(FR // 2):
            lo = max(0, 2 * p - 2)
            pre2 = jnp.dot(
                taps_of(src, range(lo, 2 * p + 2), cells),
                pair_kernel(wz, l * step, 0 if p else 2),
                preferred_element_type=F32,
            )
            for e in range(2):
                t = 2 * p + e
                pre = pre2[:, e * CH : (e + 1) * CH]
                s = jax.nn.sigmoid(pre)
                if l + 1 < LAYERS:
                    new = src[t * 3 + 1, COLS : COLS + cells].astype(F32) + pre * s
                    new = jnp.where(valid, new, 0.0).astype(BF16).astype(F32)
                    for lag_c, v in enumerate(shifted(new)):
                        dst[t * 3 + lag_c, :cells] = v
                s, pre = s[keep], pre[keep]
                slope = s * (1.0 + pre * (1.0 - s))
                if l + 1 < LAYERS:
                    fac[l, t, :kept] = slope
                else:
                    set_delta(l, t, grad[t] * slope, dst)

    for l in reversed(range(1, LAYERS)):
        cells = (OWN + 2 * (l - 1)) * COLS
        src, dst = cols.at[(l + 1) % 2], cols.at[l % 2]
        for pairs in ((0, 1, 2), (3,)):
            hi = 4 if len(pairs) > 1 else 2
            lhs = [taps_of(src, range(2 * p, 2 * p + hi), cells) for p in pairs]
            kernel = pair_kernel(wb, (l - 1) * step, 0)[: hi * PLANE]
            adjoint = jnp.dot(jnp.concatenate(lhs, 0), kernel, preferred_element_type=F32)
            for i, p in enumerate(pairs):
                for e in range(2):
                    t = 2 * p + e
                    mine_of = adjoint[i * cells : (i + 1) * cells, e * CH : (e + 1) * CH]
                    new = grad[t, COLS : COLS + cells] + mine_of
                    new = new.astype(BF16).astype(F32)
                    if l > 1:
                        grad[t, :cells] = new
                    set_delta(l - 1, t, new * fac[l - 1, t, :cells], dst)

    for d, lo, out in ((0, 0, o0), (1, 0, o1), (2, 0, oa), (2, PART // 2, ob), (3, 0, o3)):
        out[...] = part[lax.rem(seg + d, LAYERS), lo : lo + out.shape[0]]


def kernel_grad_kernel(pos, e0, e1, e3, ea, eb, keep, send, e2, x9, d3, wg):
    tm = pos[1]
    e2[: PART // 2] = ea[...]
    e2[PART // 2 :] = eb[...]
    cells = OWN * COLS
    width = cells + 2 * COLS
    nothing = jnp.zeros((cells, CH), BF16)
    for m, e in enumerate((e0, e1, e2, e3)):
        for t in range(FR):
            at = (m * FR + t) * cells
            frame = e[t * width : (t + 1) * width].astype(F32)
            for lag_c, v in enumerate(shifted(frame)):
                for lag_r in range(3):
                    tap = (lag_r * 3 + lag_c) * CH
                    x9[at : at + cells, tap : tap + CH] = v[lag_r * COLS : lag_r * COLS + cells]
            for lag_t in range(3):
                src = t + 2 - lag_t
                row = HID + src * cells
                d3[at : at + cells, lag_t * CH : (lag_t + 1) * CH] = (
                    e[row : row + cells] if src < FR else nothing
                )
    out = lax.dot_general(
        d3[...], x9[...], (((0,), (0,)), ((), ())), preferred_element_type=F32
    )
    for lag_t in range(3):
        for tap in range(9):
            at = (lag_t * 9 + tap) * CH
            wg[at : at + CH] = out[lag_t * CH : (lag_t + 1) * CH, tap * CH : (tap + 1) * CH].T
    keep[...] = wg[pl.ds(pl.multiple_of(tm * HALF, CH // 2), HALF)]
    send[...] = wg[pl.ds(pl.multiple_of((1 - tm) * HALF, CH // 2), HALF)].astype(BF16)


def edges_kernel(pos, mine, other, long, short, start):
    tm = pos[1]
    start[0] = 0
    half_fr = FR // 2
    few = HALO - OWN
    band = 2 * OWN
    for i, ref in enumerate((mine, other)):
        for t in range(half_fr):
            side = i * half_fr + t
            long[side, :HALO] = ref[t, pl.ds((1 - tm) * (band - HALO), HALO)]
            long[side, HALO:] = ref[t, pl.ds(band + (1 - tm) * (band - CHALO), CHALO)]
            short[side] = ref[t, pl.ds(tm * (band - few), few)]


def run_edges(pos, mine, other):
    return pl.pallas_call(
        edges_kernel,
        out_shape=(
            jax.ShapeDtypeStruct((FR, HALO + CHALO, COLS, CH), BF16),
            jax.ShapeDtypeStruct((FR, HALO - OWN, COLS, CH), BF16),
            jax.ShapeDtypeStruct((1,), jnp.int32),
        ),
        in_specs=in_vmem(2),
        out_specs=(pl.BlockSpec(memory_space=pltpu.VMEM),) * 2
        + (pl.BlockSpec(memory_space=pltpu.SMEM),),
        compiler_params=pltpu.CompilerParams(vmem_limit_bytes=8 * 2**20),
        cost_estimate=pl.CostEstimate(flops=0, bytes_accessed=900_000, transcendentals=0),
        name="edges",
    )(pos, mine, other)


def in_vmem(n):
    return [pl.BlockSpec(memory_space=pltpu.SMEM)] + [pl.BlockSpec(memory_space=pltpu.VMEM)] * n


def run_layers(total, pos, *arrays):
    span = OWN + 2 * HALO
    lengths = (PART, PART, PART // 2, PART // 2, PART)
    return pl.pallas_call(
        functools.partial(layers_kernel, total),
        out_shape=tuple(jax.ShapeDtypeStruct((n, CH), BF16) for n in lengths),
        in_specs=in_vmem(len(arrays)),
        out_specs=(pl.BlockSpec(memory_space=pltpu.VMEM),) * len(lengths),
        scratch_shapes=[
            pltpu.VMEM((PLANE + LAYERS * (PLANE + KC), CH), BF16),
            pltpu.VMEM((PLANE + (LAYERS - 1) * (PLANE + KC), CH), BF16),
            pltpu.VMEM((2, FR * 3, span * COLS, CH), BF16),
            pltpu.VMEM((LAYERS - 1, FR, (OWN + 2 * CHALO) * COLS, CH), F32),
            pltpu.VMEM((FR, (OWN + 2 * CHALO) * COLS, CH), F32),
            pltpu.VMEM((LAYERS, PART, CH), BF16),
        ],
        compiler_params=pltpu.CompilerParams(vmem_limit_bytes=28 * 2**20),
        cost_estimate=pl.CostEstimate(
            flops=9_000_000_000, bytes_accessed=6_000_000, transcendentals=1_000_000
        ),
        name="layers",
    )(pos, *arrays)


def run_kernel_grad(pos, *arrays):
    cells = LAYERS * FR * OWN * COLS
    return pl.pallas_call(
        kernel_grad_kernel,
        out_shape=(
            jax.ShapeDtypeStruct((HALF, CH), F32),
            jax.ShapeDtypeStruct((HALF, CH), BF16),
        ),
        in_specs=in_vmem(len(arrays)),
        out_specs=(pl.BlockSpec(memory_space=pltpu.VMEM),) * 2,
        scratch_shapes=[
            pltpu.VMEM((PART, CH), BF16),
            pltpu.VMEM((cells, PLANE), BF16),
            pltpu.VMEM((cells, 3 * CH), BF16),
            pltpu.VMEM((KC, CH), F32),
        ],
        compiler_params=pltpu.CompilerParams(vmem_limit_bytes=24 * 2**20),
        cost_estimate=pl.CostEstimate(
            flops=1_800_000_000, bytes_accessed=4_000_000, transcendentals=0
        ),
        name="kernel_grad",
    )(pos, *arrays)


def ring(count, by):
    return [(i, (i + by) % count) for i in range(count)]


def along(x, by):
    return lax.ppermute(x, "segment", ring(LAYERS, by))


def swap(x):
    return lax.ppermute(x, "tm", [(0, 1), (1, 0)])


def body(inputs, weights, cotangent):
    seg, tm = lax.axis_index("segment"), lax.axis_index("tm")
    space = lax.axis_index(("z", "y"))
    spaces = lax.axis_size(("z", "y"))
    ny, nz = lax.axis_size("y"), lax.axis_size("z")
    rows = inputs.shape[2]
    pos = jnp.stack([seg, tm, space * rows + tm * OWN]).astype(jnp.int32)

    w = weights[0]
    half = lax.dynamic_slice_in_dim(w, tm * HALF, HALF, 0)
    left, right = along(half, 1), along(half, -1)

    x = lax.dynamic_index_in_dim(inputs, seg, 0, keepdims=False)
    c = lax.dynamic_index_in_dim(cotangent, seg, 0, keepdims=False)
    mine = jnp.concatenate([x, c], 1)
    other = swap(mine)
    long, short, start = run_edges(pos, mine, other)
    down = [(i, i + 1) for i in range(spaces - 1)]
    up = [(i + 1, i) for i in range(spaces - 1)]
    both = lambda low, high: low + [(spaces + i, spaces + j) for i, j in high]
    long = lax.ppermute(long, ("tm", "z", "y"), both(down, up))
    short = lax.ppermute(short, ("tm", "z", "y"), both(up, down))

    cut = lambda v, at: lax.dynamic_slice_in_dim(v, at + start[0], HALF // 2, 0)
    got = [left, right, along(cut(left, 0), 1), along(cut(right, HALF // 2), -1)]
    crossed = [swap(g) for g in got]

    parts = run_layers(spaces * rows, pos, mine, other, long, short, w, *got, *crossed)
    far_a, far_b = along(parts[2], 1), along(parts[3], -1)
    near = [along(parts[1], 1), along(parts[4], -1)]
    keep, send = run_kernel_grad(pos, parts[0], *near, along(far_a, 1), along(far_b, -1))

    total = (keep + swap(send).astype(F32)).astype(BF16)
    rows_y = HALF // ny
    pieces = lax.all_to_all(total.reshape(ny, rows_y, CH), "y", 0, 0)
    total = jnp.sum(pieces.astype(F32), 0).astype(BF16)
    rows_z = -(-rows_y // (16 * nz)) * 16
    total = jnp.pad(total, ((0, nz * rows_z - rows_y), (0, 0)))
    pieces = lax.all_to_all(total.reshape(nz, rows_z, CH), "z", 0, 0)
    total = jnp.sum(pieces.astype(F32), 0).astype(BF16)
    whole = lax.all_to_all(jnp.broadcast_to(total, (nz, rows_z, CH)), "z", 0, 0)
    whole = whole.reshape(nz * rows_z, CH)[:rows_y]
    whole = lax.all_to_all(jnp.broadcast_to(whole, (ny, rows_y, CH)), "y", 0, 0)
    whole = whole.reshape(HALF, CH)
    theirs = swap(whole)
    low = jnp.where(tm == 0, whole, theirs)
    high = jnp.where(tm == 0, theirs, whole)
    return jnp.concatenate([low, high], 0).astype(F32)[None]


def solution(mesh):
    segments, cores, spaces = mesh.devices.shape
    ny = 4 if spaces % 4 == 0 else 1
    fine = Mesh(
        mesh.devices.reshape(segments, cores, spaces // ny, ny), ("segment", "tm", "z", "y")
    )
    spec = P(None, "tm", ("z", "y"), None, None)
    return jax.shard_map(
        body,
        mesh=fine,
        in_specs=(spec, P("segment", None, None), spec),
        out_specs=P("segment", None, None),
        check_vma=False,
    )
```

```python
import functools

import jax
import jax.numpy as jnp
from jax import lax
from jax.experimental import pallas as pl
from jax.experimental.pallas import tpu as pltpu
from jax.sharding import Mesh
from jax.sharding import PartitionSpec as P

BF16 = jnp.bfloat16
F32 = jnp.float32
CH = 128
COLS = 16
FR = 8
LAYERS = 4
TAPS = 27
KC = TAPS * CH
HALF = KC // 2
PLANE = 9 * CH
OWN = 4
HALO = 7
CHALO = 3
HID = FR * (OWN + 2) * COLS
PART = HID + FR * OWN * COLS


def shifted(x):
    cells = x.shape[0]
    col = lax.broadcasted_iota(jnp.int32, x.shape, 0) % COLS
    before = jnp.where(col == 0, 0.0, pltpu.roll(x, 1, 0))
    after = jnp.where(col == COLS - 1, 0.0, pltpu.roll(x, cells - 1, 0))
    return before.astype(BF16), x.astype(BF16), after.astype(BF16)


def inside(first, rows, total):
    row = first + lax.broadcasted_iota(jnp.int32, (rows * COLS, CH), 0) // COLS
    return (row >= 0) & (row < total)


def taps_of(cols, frames, cells):
    return jnp.concatenate(
        [
            cols[t * 3 + lag_c, lag_r * COLS : lag_r * COLS + cells]
            for t in frames
            for lag_r in range(3)
            for lag_c in range(3)
        ],
        1,
    )


def pair_kernel(ref, base, first):
    rows = (4 - first) * PLANE
    at = base + first * PLANE
    return jnp.concatenate(
        [ref[pl.ds(at + PLANE, rows)], ref[pl.ds(at, rows)]],
        1,
    )


def layers_kernel(
    total, pos, mine, other, long, short, w0, r1, r3, ra, rb, q1, q3, qa, qb, *rest
):
    o0, o1, oa, ob, o3, wz, wb, cols, fac, grad, part = rest
    seg, tm, first = pos[0], pos[1], pos[2]
    step = PLANE + KC
    zero = jnp.zeros((PLANE, CH), BF16)
    for l in range(LAYERS + 1):
        wz[l * step : l * step + PLANE] = zero
    for l in range(LAYERS):
        wb[l * step : l * step + PLANE] = zero
    wz[pl.ds(pl.multiple_of(seg * step + PLANE, CH), KC)] = w0[...]
    for d, skip, r, q in ((1, 0, r1, q1), (3, 0, r3, q3), (2, 0, ra, qa), (2, HALF // 2, rb, qb)):
        at = lax.rem(seg + LAYERS - d, LAYERS) * step + PLANE + skip
        for ref, half in ((r, tm), (q, 1 - tm)):
            wz[pl.ds(pl.multiple_of(at + half * HALF, 32), ref.shape[0])] = ref[...]

    span = OWN + 2 * HALO
    half_fr = FR // 2
    band = 2 * OWN
    near = HALO - OWN
    upper = 1 - tm

    def put(t, to, rows):
        cells = rows.shape[0] * COLS
        at = pl.multiple_of(to * COLS, COLS)
        cols[0, t * 3 + 1, pl.ds(at, cells)] = rows.reshape(cells, CH)

    def put_grad(t, to, rows):
        cells = rows.shape[0] * COLS
        at = pl.multiple_of(to * COLS, COLS)
        grad[t, pl.ds(at, cells)] = rows.reshape(cells, CH).astype(F32)

    for i, (ref, which) in enumerate(((mine, tm), (other, upper))):

        @pl.loop(0, half_fr)
        def _(t):
            frame = which * half_fr + t
            side = i * half_fr + t
            put(frame, tm * (near + band), long[side, :HALO])
            put(frame, near + upper * OWN, ref[t, :band])
            put(frame, upper * (HALO + band), short[side])
            for lag_c, v in enumerate(shifted(cols[0, frame * 3 + 1].astype(F32))):
                if lag_c != 1:
                    cols[0, frame * 3 + lag_c] = v
            rest_rows = band - 1
            put_grad(frame, upper * CHALO, ref[t, pl.ds(band + tm, rest_rows)])
            put_grad(frame, tm * rest_rows, long[side, HALO:])

    width = (OWN + 2) * COLS
    own_cells = OWN * COLS

    def set_delta(l, t, value, to):
        cells = value.shape[0]
        valid = inside(first - l, OWN + 2 * l, total)
        delta = jnp.where(valid, value, 0.0).astype(BF16)
        at = HID + t * own_cells
        part[l, at : at + own_cells] = delta[l * COLS : l * COLS + own_cells]
        if l > 0:
            for lag_c, v in enumerate(shifted(delta.astype(F32))):
                to[t * 3 + lag_c, :cells] = v

    for l in range(LAYERS):
        rows = span - 2 * (l + 1)
        cells = rows * COLS
        src, dst = cols.at[l % 2], cols.at[(l + 1) % 2]
        for t in range(FR):
            at = (6 - l) * COLS
            part[l, t * width : (t + 1) * width] = src[t * 3 + 1, at : at + width]
        if l > 0:
            for k in range(TAPS):
                at = l * step + PLANE + (TAPS - 1 - k) * CH
                to = (l - 1) * step + PLANE + k * CH
                wb[to : to + CH] = wz[at : at + CH].T
        keep = slice((6 - 2 * l) * COLS, 10 * COLS)
        kept = (OWN + 2 * l) * COLS
        valid = inside(first - HALO + l + 1, rows, total)
        for p in range(FR // 2):
            lo = max(0, 2 * p - 2)
            pre2 = jnp.dot(
                taps_of(src, range(lo, 2 * p + 2), cells),
                pair_kernel(wz, l * step, 0 if p else 2),
                preferred_element_type=F32,
            )
            for e in range(2):
                t = 2 * p + e
                pre = pre2[:, e * CH : (e + 1) * CH]
                s = jax.nn.sigmoid(pre)
                if l + 1 < LAYERS:
                    new = src[t * 3 + 1, COLS : COLS + cells].astype(F32) + pre * s
                    new = jnp.where(valid, new, 0.0).astype(BF16).astype(F32)
                    for lag_c, v in enumerate(shifted(new)):
                        dst[t * 3 + lag_c, :cells] = v
                s, pre = s[keep], pre[keep]
                slope = s * (1.0 + pre * (1.0 - s))
                if l + 1 < LAYERS:
                    fac[l, t, :kept] = slope
                else:
                    set_delta(l, t, grad[t] * slope, dst)

    for l in reversed(range(1, LAYERS)):
        cells = (OWN + 2 * (l - 1)) * COLS
        src, dst = cols.at[(l + 1) % 2], cols.at[l % 2]
        for pairs in ((0, 1, 2), (3,)):
            hi = 4 if len(pairs) > 1 else 2
            lhs = [taps_of(src, range(2 * p, 2 * p + hi), cells) for p in pairs]
            kernel = pair_kernel(wb, (l - 1) * step, 0)[: hi * PLANE]
            adjoint = jnp.dot(jnp.concatenate(lhs, 0), kernel, preferred_element_type=F32)
            for i, p in enumerate(pairs):
                for e in range(2):
                    t = 2 * p + e
                    mine_of = adjoint[i * cells : (i + 1) * cells, e * CH : (e + 1) * CH]
                    new = grad[t, COLS : COLS + cells] + mine_of
                    new = new.astype(BF16).astype(F32)
                    if l > 1:
                        grad[t, :cells] = new
                    set_delta(l - 1, t, new * fac[l - 1, t, :cells], dst)

    for d, lo, out in ((0, 0, o0), (1, 0, o1), (2, 0, oa), (2, PART // 2, ob), (3, 0, o3)):
        out[...] = part[lax.rem(seg + d, LAYERS), lo : lo + out.shape[0]]


def kernel_grad_kernel(pos, e0, e1, e3, ea, eb, keep, send, e2, x9, d3, wg):
    tm = pos[1]
    e2[: PART // 2] = ea[...]
    e2[PART // 2 :] = eb[...]
    cells = OWN * COLS
    width = cells + 2 * COLS
    nothing = jnp.zeros((cells, CH), BF16)
    for m, e in enumerate((e0, e1, e2, e3)):
        for t in range(FR):
            at = (m * FR + t) * cells
            frame = e[t * width : (t + 1) * width].astype(F32)
            for lag_c, v in enumerate(shifted(frame)):
                for lag_r in range(3):
                    tap = (lag_r * 3 + lag_c) * CH
                    x9[at : at + cells, tap : tap + CH] = v[lag_r * COLS : lag_r * COLS + cells]
            for lag_t in range(3):
                src = t + 2 - lag_t
                row = HID + src * cells
                d3[at : at + cells, lag_t * CH : (lag_t + 1) * CH] = (
                    e[row : row + cells] if src < FR else nothing
                )
    out = lax.dot_general(
        d3[...], x9[...], (((0,), (0,)), ((), ())), preferred_element_type=F32
    )
    for lag_t in range(3):
        for tap in range(9):
            at = (lag_t * 9 + tap) * CH
            wg[at : at + CH] = out[lag_t * CH : (lag_t + 1) * CH, tap * CH : (tap + 1) * CH].T
    keep[...] = wg[pl.ds(pl.multiple_of(tm * HALF, CH // 2), HALF)]
    send[...] = wg[pl.ds(pl.multiple_of((1 - tm) * HALF, CH // 2), HALF)].astype(BF16)


def edges_kernel(pos, mine, other, long, short):
    tm = pos[1]
    half_fr = FR // 2
    few = HALO - OWN
    band = 2 * OWN
    for i, ref in enumerate((mine, other)):
        for t in range(half_fr):
            side = i * half_fr + t
            long[side, :HALO] = ref[t, pl.ds((1 - tm) * (band - HALO), HALO)]
            long[side, HALO:] = ref[t, pl.ds(band + (1 - tm) * (band - CHALO), CHALO)]
            short[side] = ref[t, pl.ds(tm * (band - few), few)]


def run_edges(pos, mine, other):
    return pl.pallas_call(
        edges_kernel,
        out_shape=(
            jax.ShapeDtypeStruct((FR, HALO + CHALO, COLS, CH), BF16),
            jax.ShapeDtypeStruct((FR, HALO - OWN, COLS, CH), BF16),
        ),
        in_specs=in_vmem(2),
        out_specs=(pl.BlockSpec(memory_space=pltpu.VMEM),) * 2,
        compiler_params=pltpu.CompilerParams(vmem_limit_bytes=8 * 2**20),
        cost_estimate=pl.CostEstimate(flops=0, bytes_accessed=900_000, transcendentals=0),
        name="edges",
    )(pos, mine, other)


def zero_kernel(after, start):
    del after
    start[0] = 0


def zero_after(x):
    return pl.pallas_call(
        zero_kernel,
        out_shape=jax.ShapeDtypeStruct((1,), jnp.int32),
        in_specs=[pl.BlockSpec(memory_space=pltpu.VMEM)],
        out_specs=pl.BlockSpec(memory_space=pltpu.SMEM),
        compiler_params=pltpu.CompilerParams(vmem_limit_bytes=4 * 2**20),
        name="zero_after",
    )(x)[0]


def in_vmem(n):
    return [pl.BlockSpec(memory_space=pltpu.SMEM)] + [pl.BlockSpec(memory_space=pltpu.VMEM)] * n


def run_layers(total, pos, *arrays):
    span = OWN + 2 * HALO
    lengths = (PART, PART, PART // 2, PART // 2, PART)
    return pl.pallas_call(
        functools.partial(layers_kernel, total),
        out_shape=tuple(jax.ShapeDtypeStruct((n, CH), BF16) for n in lengths),
        in_specs=in_vmem(len(arrays)),
        out_specs=(pl.BlockSpec(memory_space=pltpu.VMEM),) * len(lengths),
        scratch_shapes=[
            pltpu.VMEM((PLANE + LAYERS * (PLANE + KC), CH), BF16),
            pltpu.VMEM((PLANE + (LAYERS - 1) * (PLANE + KC), CH), BF16),
            pltpu.VMEM((2, FR * 3, span * COLS, CH), BF16),
            pltpu.VMEM((LAYERS - 1, FR, (OWN + 2 * CHALO) * COLS, CH), F32),
            pltpu.VMEM((FR, (OWN + 2 * CHALO) * COLS, CH), F32),
            pltpu.VMEM((LAYERS, PART, CH), BF16),
        ],
        compiler_params=pltpu.CompilerParams(vmem_limit_bytes=28 * 2**20),
        cost_estimate=pl.CostEstimate(
            flops=9_000_000_000, bytes_accessed=6_000_000, transcendentals=1_000_000
        ),
        name="layers",
    )(pos, *arrays)


def run_kernel_grad(pos, *arrays):
    cells = LAYERS * FR * OWN * COLS
    return pl.pallas_call(
        kernel_grad_kernel,
        out_shape=(
            jax.ShapeDtypeStruct((HALF, CH), F32),
            jax.ShapeDtypeStruct((HALF, CH), BF16),
        ),
        in_specs=in_vmem(len(arrays)),
        out_specs=(pl.BlockSpec(memory_space=pltpu.VMEM),) * 2,
        scratch_shapes=[
            pltpu.VMEM((PART, CH), BF16),
            pltpu.VMEM((cells, PLANE), BF16),
            pltpu.VMEM((cells, 3 * CH), BF16),
            pltpu.VMEM((KC, CH), F32),
        ],
        compiler_params=pltpu.CompilerParams(vmem_limit_bytes=24 * 2**20),
        cost_estimate=pl.CostEstimate(
            flops=1_800_000_000, bytes_accessed=4_000_000, transcendentals=0
        ),
        name="kernel_grad",
    )(pos, *arrays)


def ring(count, by):
    return [(i, (i + by) % count) for i in range(count)]


def along(x, by):
    return lax.ppermute(x, "segment", ring(LAYERS, by))


def swap(x):
    return lax.ppermute(x, "tm", [(0, 1), (1, 0)])


def body(inputs, weights, cotangent):
    seg, tm = lax.axis_index("segment"), lax.axis_index("tm")
    space = lax.axis_index(("z", "y"))
    spaces = lax.axis_size(("z", "y"))
    ny, nz = lax.axis_size("y"), lax.axis_size("z")
    rows = inputs.shape[2]
    pos = jnp.stack([seg, tm, space * rows + tm * OWN]).astype(jnp.int32)

    w = weights[0]
    half = lax.dynamic_slice_in_dim(w, tm * HALF, HALF, 0)
    left, right = along(half, 1), along(half, -1)

    x = lax.dynamic_index_in_dim(inputs, seg, 0, keepdims=False)
    c = lax.dynamic_index_in_dim(cotangent, seg, 0, keepdims=False)
    mine = jnp.concatenate([x, c], 1)
    other = swap(mine)
    long, short = run_edges(pos, mine, other)
    down = [(i, i + 1) for i in range(spaces - 1)]
    up = [(i + 1, i) for i in range(spaces - 1)]
    both = lambda low, high: low + [(spaces + i, spaces + j) for i, j in high]
    long = lax.ppermute(long, ("tm", "z", "y"), both(down, up))
    short = lax.ppermute(short, ("tm", "z", "y"), both(up, down))

    start = zero_after(short)
    late = zero_after(long)
    cut = lambda v, at: lax.dynamic_slice_in_dim(v, at + start, HALF // 2, 0)
    got = [left, right, along(cut(left, 0), 1), along(cut(right, HALF // 2), -1)]
    held = [lax.dynamic_slice_in_dim(jnp.pad(g, ((0, 16), (0, 0))), late, HALF // 2, 0) for g in got[2:]]
    crossed = [swap(g) for g in got[:2] + held]

    parts = run_layers(spaces * rows, pos, mine, other, long, short, w, *got, *crossed)
    far_a, far_b = along(parts[2], 1), along(parts[3], -1)
    near = [along(parts[1], 1), along(parts[4], -1)]
    keep, send = run_kernel_grad(pos, parts[0], *near, along(far_a, 1), along(far_b, -1))

    total = (keep + swap(send).astype(F32)).astype(BF16)
    rows_y = HALF // ny
    pieces = lax.all_to_all(total.reshape(ny, rows_y, CH), "y", 0, 0)
    total = jnp.sum(pieces.astype(F32), 0).astype(BF16)
    rows_z = -(-rows_y // (16 * nz)) * 16
    total = jnp.pad(total, ((0, nz * rows_z - rows_y), (0, 0)))
    pieces = lax.all_to_all(total.reshape(nz, rows_z, CH), "z", 0, 0)
    total = jnp.sum(pieces.astype(F32), 0).astype(BF16)
    whole = lax.all_to_all(jnp.broadcast_to(total, (nz, rows_z, CH)), "z", 0, 0)
    whole = whole.reshape(nz * rows_z, CH)[:rows_y]
    whole = lax.all_to_all(jnp.broadcast_to(whole, (ny, rows_y, CH)), "y", 0, 0)
    whole = whole.reshape(HALF, CH)
    theirs = swap(whole)
    low = jnp.where(tm == 0, whole, theirs)
    high = jnp.where(tm == 0, theirs, whole)
    return jnp.concatenate([low, high], 0).astype(F32)[None]


def solution(mesh):
    segments, cores, spaces = mesh.devices.shape
    ny = 4 if spaces % 4 == 0 else 1
    fine = Mesh(
        mesh.devices.reshape(segments, cores, spaces // ny, ny), ("segment", "tm", "z", "y")
    )
    spec = P(None, "tm", ("z", "y"), None, None)
    return jax.shard_map(
        body,
        mesh=fine,
        in_specs=(spec, P("segment", None, None), spec),
        out_specs=P("segment", None, None),
        check_vma=False,
    )
```

```python
import functools

import jax
import jax.numpy as jnp
from jax import lax
from jax.experimental import pallas as pl
from jax.experimental.pallas import tpu as pltpu
from jax.sharding import Mesh
from jax.sharding import PartitionSpec as P

BF16 = jnp.bfloat16
F32 = jnp.float32
CH = 128
COLS = 16
FR = 8
LAYERS = 4
TAPS = 27
KC = TAPS * CH
HALF = KC // 2
PLANE = 9 * CH
OWN = 4
HALO = 7
CHALO = 3
HID = FR * (OWN + 2) * COLS
PART = HID + FR * OWN * COLS


def shifted(x):
    cells = x.shape[0]
    col = lax.broadcasted_iota(jnp.int32, x.shape, 0) % COLS
    before = jnp.where(col == 0, 0.0, pltpu.roll(x, 1, 0))
    after = jnp.where(col == COLS - 1, 0.0, pltpu.roll(x, cells - 1, 0))
    return before.astype(BF16), x.astype(BF16), after.astype(BF16)


def inside(first, rows, total):
    row = first + lax.broadcasted_iota(jnp.int32, (rows * COLS, CH), 0) // COLS
    return (row >= 0) & (row < total)


def taps_of(cols, frames, cells):
    return jnp.concatenate(
        [
            cols[t * 3 + lag_c, lag_r * COLS : lag_r * COLS + cells]
            for t in frames
            for lag_r in range(3)
            for lag_c in range(3)
        ],
        1,
    )


def pair_kernel(ref, base, first):
    rows = (4 - first) * PLANE
    at = base + first * PLANE
    return jnp.concatenate(
        [ref[pl.ds(at + PLANE, rows)], ref[pl.ds(at, rows)]],
        1,
    )


def layers_kernel(
    total, pos, mine, other, w0, r1, r3, ra, rb, q1, q3, qa, qb, *rest
):
    o0, o1, oa, ob, o3, wz, wb, cols, fac, grad, part = rest
    seg, tm, first = pos[0], pos[1], pos[2]
    step = PLANE + KC
    zero = jnp.zeros((PLANE, CH), BF16)
    for l in range(LAYERS + 1):
        wz[l * step : l * step + PLANE] = zero
    for l in range(LAYERS):
        wb[l * step : l * step + PLANE] = zero
    wz[pl.ds(pl.multiple_of(seg * step + PLANE, CH), KC)] = w0[...]
    for d, skip, r, q in ((1, 0, r1, q1), (3, 0, r3, q3), (2, 0, ra, qa), (2, HALF // 2, rb, qb)):
        at = lax.rem(seg + LAYERS - d, LAYERS) * step + PLANE + skip
        for ref, half in ((r, tm), (q, 1 - tm)):
            wz[pl.ds(pl.multiple_of(at + half * HALF, 32), ref.shape[0])] = ref[...]

    span = OWN + 2 * HALO
    half_fr = FR // 2
    for ref, which in ((mine, tm), (other, 1 - tm)):

        @pl.loop(0, half_fr)
        def _(t):
            frame = which * half_fr + t
            rows = ref[t, pl.ds(tm * OWN, span)]
            for lag_c, v in enumerate(shifted(rows.reshape(span * COLS, CH).astype(F32))):
                cols[0, frame * 3 + lag_c] = v
            at = 2 * HALO + 2 * OWN + tm * OWN
            rows = ref[t, pl.ds(at, OWN + 2 * CHALO)]
            grad[frame] = rows.reshape(-1, CH).astype(F32)

    width = (OWN + 2) * COLS
    own_cells = OWN * COLS

    def set_delta(l, t, value, to):
        cells = value.shape[0]
        valid = inside(first - l, OWN + 2 * l, total)
        delta = jnp.where(valid, value, 0.0).astype(BF16)
        at = HID + t * own_cells
        part[l, at : at + own_cells] = delta[l * COLS : l * COLS + own_cells]
        if l > 0:
            for lag_c, v in enumerate(shifted(delta.astype(F32))):
                to[t * 3 + lag_c, :cells] = v

    for l in range(LAYERS):
        rows = span - 2 * (l + 1)
        cells = rows * COLS
        src, dst = cols.at[l % 2], cols.at[(l + 1) % 2]
        for t in range(FR):
            at = (6 - l) * COLS
            part[l, t * width : (t + 1) * width] = src[t * 3 + 1, at : at + width]
        if l > 0:
            for k in range(TAPS):
                at = l * step + PLANE + (TAPS - 1 - k) * CH
                to = (l - 1) * step + PLANE + k * CH
                wb[to : to + CH] = wz[at : at + CH].T
        keep = slice((6 - 2 * l) * COLS, 10 * COLS)
        kept = (OWN + 2 * l) * COLS
        valid = inside(first - HALO + l + 1, rows, total)
        for p in range(FR // 2):
            lo = max(0, 2 * p - 2)
            pre2 = jnp.dot(
                taps_of(src, range(lo, 2 * p + 2), cells),
                pair_kernel(wz, l * step, 0 if p else 2),
                preferred_element_type=F32,
            )
            for e in range(2):
                t = 2 * p + e
                pre = pre2[:, e * CH : (e + 1) * CH]
                s = jax.nn.sigmoid(pre)
                if l + 1 < LAYERS:
                    new = src[t * 3 + 1, COLS : COLS + cells].astype(F32) + pre * s
                    new = jnp.where(valid, new, 0.0).astype(BF16).astype(F32)
                    for lag_c, v in enumerate(shifted(new)):
                        dst[t * 3 + lag_c, :cells] = v
                s, pre = s[keep], pre[keep]
                slope = s * (1.0 + pre * (1.0 - s))
                if l + 1 < LAYERS:
                    fac[l, t, :kept] = slope
                else:
                    set_delta(l, t, grad[t] * slope, dst)

    for l in reversed(range(1, LAYERS)):
        cells = (OWN + 2 * (l - 1)) * COLS
        src, dst = cols.at[(l + 1) % 2], cols.at[l % 2]
        for pairs in ((0, 1, 2), (3,)):
            hi = 4 if len(pairs) > 1 else 2
            lhs = [taps_of(src, range(2 * p, 2 * p + hi), cells) for p in pairs]
            kernel = pair_kernel(wb, (l - 1) * step, 0)[: hi * PLANE]
            adjoint = jnp.dot(jnp.concatenate(lhs, 0), kernel, preferred_element_type=F32)
            for i, p in enumerate(pairs):
                for e in range(2):
                    t = 2 * p + e
                    mine_of = adjoint[i * cells : (i + 1) * cells, e * CH : (e + 1) * CH]
                    new = grad[t, COLS : COLS + cells] + mine_of
                    new = new.astype(BF16).astype(F32)
                    if l > 1:
                        grad[t, :cells] = new
                    set_delta(l - 1, t, new * fac[l - 1, t, :cells], dst)

    for d, lo, out in ((0, 0, o0), (1, 0, o1), (2, 0, oa), (2, PART // 2, ob), (3, 0, o3)):
        out[...] = part[lax.rem(seg + d, LAYERS), lo : lo + out.shape[0]]


def kernel_grad_kernel(pos, e0, e1, e3, ea, eb, keep, send, e2, cols, deltas, wg):
    tm = pos[1]
    e2[: PART // 2] = ea[...]
    e2[PART // 2 :] = eb[...]
    cells = OWN * COLS
    width = cells + 2 * COLS
    total = LAYERS * FR * cells
    for m, e in enumerate((e0, e1, e2, e3)):
        for t in range(FR):
            frame = e[t * width : (t + 1) * width]
            before, _, after = shifted(frame.astype(F32))
            for lag_c, v in enumerate((before, frame, after)):
                cols[lag_c, m * FR + t] = v
            deltas[m, t] = e[HID + t * cells : HID + (t + 1) * cells]
        for t in (FR, FR + 1):
            deltas[m, t] = jnp.zeros((cells, CH), BF16)
    x9 = jnp.concatenate(
        [
            cols[lag_c, :, lag_r * COLS : lag_r * COLS + cells].reshape(total, CH)
            for lag_r in range(3)
            for lag_c in range(3)
        ],
        1,
    )
    d3 = jnp.concatenate(
        [deltas[:, 2 - lag_t : 2 - lag_t + FR].reshape(total, CH) for lag_t in range(3)], 1
    )
    out = lax.dot_general(d3, x9, (((0,), (0,)), ((), ())), preferred_element_type=F32)
    for lag_t in range(3):
        for tap in range(9):
            at = (lag_t * 9 + tap) * CH
            wg[at : at + CH] = out[lag_t * CH : (lag_t + 1) * CH, tap * CH : (tap + 1) * CH].T
    keep[...] = wg[pl.ds(pl.multiple_of(tm * HALF, CH // 2), HALF)]
    send[...] = wg[pl.ds(pl.multiple_of((1 - tm) * HALF, CH // 2), HALF)].astype(BF16)


def zero_kernel(*refs):
    refs[-1][0] = 0


def zero_after(*arrays):
    return pl.pallas_call(
        zero_kernel,
        out_shape=jax.ShapeDtypeStruct((1,), jnp.int32),
        in_specs=[pl.BlockSpec(memory_space=pltpu.VMEM)] * len(arrays),
        out_specs=pl.BlockSpec(memory_space=pltpu.SMEM),
        compiler_params=pltpu.CompilerParams(vmem_limit_bytes=4 * 2**20),
        name="zero_after",
    )(*arrays)


def join_kernel(start, before, after, x, c, out):
    at = start[0]
    rows = x.shape[1]
    for t in range(FR // 2):
        for to, n, ref, lo in (
            (0, HALO, before, 0),
            (HALO, rows, x, 0),
            (HALO + rows, HALO, after, 0),
            (2 * HALO + rows, CHALO, before, HALO),
            (2 * HALO + CHALO + rows, rows, c, 0),
            (2 * HALO + CHALO + 2 * rows, CHALO, after, HALO),
        ):
            out[t, pl.ds(at + to, n)] = ref[t, lo : lo + n]


def run_join(start, *arrays):
    return pl.pallas_call(
        join_kernel,
        out_shape=jax.ShapeDtypeStruct((FR // 2, 4 * OWN + 2 * HALO + 2 * CHALO, COLS, CH), BF16),
        in_specs=in_vmem(4),
        out_specs=pl.BlockSpec(memory_space=pltpu.VMEM),
        compiler_params=pltpu.CompilerParams(vmem_limit_bytes=8 * 2**20),
        name="join",
    )(start, *arrays)


def in_vmem(n):
    return [pl.BlockSpec(memory_space=pltpu.SMEM)] + [pl.BlockSpec(memory_space=pltpu.VMEM)] * n


def run_layers(total, pos, *arrays):
    span = OWN + 2 * HALO
    lengths = (PART, PART, PART // 2, PART // 2, PART)
    return pl.pallas_call(
        functools.partial(layers_kernel, total),
        out_shape=tuple(jax.ShapeDtypeStruct((n, CH), BF16) for n in lengths),
        in_specs=in_vmem(len(arrays)),
        out_specs=(pl.BlockSpec(memory_space=pltpu.VMEM),) * len(lengths),
        scratch_shapes=[
            pltpu.VMEM((PLANE + LAYERS * (PLANE + KC), CH), BF16),
            pltpu.VMEM((PLANE + (LAYERS - 1) * (PLANE + KC), CH), BF16),
            pltpu.VMEM((2, FR * 3, span * COLS, CH), BF16),
            pltpu.VMEM((LAYERS - 1, FR, (OWN + 2 * CHALO) * COLS, CH), F32),
            pltpu.VMEM((FR, (OWN + 2 * CHALO) * COLS, CH), F32),
            pltpu.VMEM((LAYERS, PART, CH), BF16),
        ],
        compiler_params=pltpu.CompilerParams(vmem_limit_bytes=28 * 2**20),
        cost_estimate=pl.CostEstimate(
            flops=9_000_000_000, bytes_accessed=6_000_000, transcendentals=1_000_000
        ),
        name="layers",
    )(pos, *arrays)


def run_kernel_grad(pos, *arrays):
    return pl.pallas_call(
        kernel_grad_kernel,
        out_shape=(
            jax.ShapeDtypeStruct((HALF, CH), F32),
            jax.ShapeDtypeStruct((HALF, CH), BF16),
        ),
        in_specs=in_vmem(len(arrays)),
        out_specs=(pl.BlockSpec(memory_space=pltpu.VMEM),) * 2,
        scratch_shapes=[
            pltpu.VMEM((PART, CH), BF16),
            pltpu.VMEM((3, LAYERS * FR, (OWN + 2) * COLS, CH), BF16),
            pltpu.VMEM((LAYERS, FR + 2, OWN * COLS, CH), BF16),
            pltpu.VMEM((KC, CH), F32),
        ],
        compiler_params=pltpu.CompilerParams(vmem_limit_bytes=24 * 2**20),
        cost_estimate=pl.CostEstimate(
            flops=1_800_000_000, bytes_accessed=4_000_000, transcendentals=0
        ),
        name="kernel_grad",
    )(pos, *arrays)


def ring(count, by):
    return [(i, (i + by) % count) for i in range(count)]


def along(x, by):
    return lax.ppermute(x, "segment", ring(LAYERS, by))


def swap(x):
    return lax.ppermute(x, "tm", [(0, 1), (1, 0)])


def body(inputs, weights, cotangent):
    seg, tm = lax.axis_index("segment"), lax.axis_index("tm")
    space = lax.axis_index(("z", "y"))
    spaces = lax.axis_size(("z", "y"))
    ny, nz = lax.axis_size("y"), lax.axis_size("z")
    rows = inputs.shape[2]
    pos = jnp.stack([seg, tm, space * rows + tm * OWN]).astype(jnp.int32)

    w = weights[0]
    half = lax.dynamic_slice_in_dim(w, tm * HALF, HALF, 0)
    left, right = along(half, 1), along(half, -1)
    got = [left, right, along(left[: HALF // 2], 1), along(right[HALF // 2 :], -1)]
    start = zero_after(*got[2:])
    crossed = [swap(g) for g in got]

    x = lax.dynamic_index_in_dim(inputs, seg, 0, keepdims=False)
    c = lax.dynamic_index_in_dim(cotangent, seg, 0, keepdims=False)
    down = [(i, i + 1) for i in range(spaces - 1)]
    up = [(i + 1, i) for i in range(spaces - 1)]
    before = lax.ppermute(
        jnp.concatenate([x[:, rows - HALO :], c[:, rows - CHALO :]], 1), ("z", "y"), down
    )
    after = lax.ppermute(jnp.concatenate([x[:, :HALO], c[:, :CHALO]], 1), ("z", "y"), up)
    mine = run_join(start, before, after, x, c)
    other = swap(mine)

    parts = run_layers(spaces * rows, pos, mine, other, w, *got, *crossed)
    far_a, far_b = along(parts[2], 1), along(parts[3], -1)
    near = [along(parts[1], 1), along(parts[4], -1)]
    keep, send = run_kernel_grad(pos, parts[0], *near, along(far_a, 1), along(far_b, -1))

    total = (keep + swap(send).astype(F32)).astype(BF16)
    rows_y = HALF // ny
    pieces = lax.all_to_all(total.reshape(ny, rows_y, CH), "y", 0, 0)
    total = jnp.sum(pieces.astype(F32), 0).astype(BF16)
    rows_z = -(-rows_y // (16 * nz)) * 16
    total = jnp.pad(total, ((0, nz * rows_z - rows_y), (0, 0)))
    pieces = lax.all_to_all(total.reshape(nz, rows_z, CH), "z", 0, 0)
    total = jnp.sum(pieces.astype(F32), 0).astype(BF16)
    whole = lax.all_to_all(jnp.broadcast_to(total, (nz, rows_z, CH)), "z", 0, 0)
    whole = whole.reshape(nz * rows_z, CH)[:rows_y]
    whole = lax.all_to_all(jnp.broadcast_to(whole, (ny, rows_y, CH)), "y", 0, 0)
    whole = whole.reshape(HALF, CH)
    theirs = swap(whole)
    low = jnp.where(tm == 0, whole, theirs)
    high = jnp.where(tm == 0, theirs, whole)
    return jnp.concatenate([low, high], 0).astype(F32)[None]


def solution(mesh):
    segments, cores, spaces = mesh.devices.shape
    ny = 4 if spaces % 4 == 0 else 1
    fine = Mesh(
        mesh.devices.reshape(segments, cores, spaces // ny, ny), ("segment", "tm", "z", "y")
    )
    spec = P(None, "tm", ("z", "y"), None, None)
    return jax.shard_map(
        body,
        mesh=fine,
        in_specs=(spec, P("segment", None, None), spec),
        out_specs=P("segment", None, None),
        check_vma=False,
    )
```

```python
import functools

import jax
import jax.numpy as jnp
from jax import lax
from jax.experimental import pallas as pl
from jax.experimental.pallas import tpu as pltpu
from jax.sharding import Mesh
from jax.sharding import PartitionSpec as P

BF16 = jnp.bfloat16
F32 = jnp.float32
CH = 128
COLS = 16
FR = 8
LAYERS = 4
TAPS = 27
KC = TAPS * CH
HALF = KC // 2
PLANE = 9 * CH
OWN = 4
HALO = 7
CHALO = 3
HID = FR * (OWN + 2) * COLS
PART = HID + FR * OWN * COLS


def shifted(x):
    cells = x.shape[0]
    col = lax.broadcasted_iota(jnp.int32, x.shape, 0) % COLS
    before = jnp.where(col == 0, 0.0, pltpu.roll(x, 1, 0))
    after = jnp.where(col == COLS - 1, 0.0, pltpu.roll(x, cells - 1, 0))
    return before.astype(BF16), x.astype(BF16), after.astype(BF16)


def inside(first, rows, total):
    row = first + lax.broadcasted_iota(jnp.int32, (rows * COLS, CH), 0) // COLS
    return (row >= 0) & (row < total)


def taps_of(cols, frames, cells):
    return jnp.concatenate(
        [
            cols[t * 3 + lag_c, lag_r * COLS : lag_r * COLS + cells]
            for t in frames
            for lag_r in range(3)
            for lag_c in range(3)
        ],
        1,
    )


def pair_kernel(ref, base, first):
    rows = (4 - first) * PLANE
    at = base + first * PLANE
    return jnp.concatenate(
        [ref[pl.ds(at + PLANE, rows)], ref[pl.ds(at, rows)]],
        1,
    )


def layers_kernel(
    total, pos, mine, other, w0, r1, r3, ra, rb, q1, q3, qa, qb, *rest
):
    part, wz, wb, cols, fac, grad = rest
    seg, tm, first = pos[0], pos[1], pos[2]
    step = PLANE + KC
    zero = jnp.zeros((PLANE, CH), BF16)
    for l in range(LAYERS + 1):
        wz[l * step : l * step + PLANE] = zero
    for l in range(LAYERS):
        wb[l * step : l * step + PLANE] = zero
    wz[pl.ds(pl.multiple_of(seg * step + PLANE, CH), KC)] = w0[...]
    for d, skip, r, q in ((1, 0, r1, q1), (3, 0, r3, q3), (2, 0, ra, qa), (2, HALF // 2, rb, qb)):
        at = lax.rem(seg + LAYERS - d, LAYERS) * step + PLANE + skip
        for ref, half in ((r, tm), (q, 1 - tm)):
            wz[pl.ds(pl.multiple_of(at + half * HALF, 32), ref.shape[0])] = ref[...]

    span = OWN + 2 * HALO
    half_fr = FR // 2
    for ref, which in ((mine, tm), (other, 1 - tm)):

        @pl.loop(0, half_fr)
        def _(t):
            frame = which * half_fr + t
            rows = ref[t, pl.ds(tm * OWN, span)]
            for lag_c, v in enumerate(shifted(rows.reshape(span * COLS, CH).astype(F32))):
                cols[0, frame * 3 + lag_c] = v
            at = 2 * HALO + 2 * OWN + tm * OWN
            rows = ref[t, pl.ds(at, OWN + 2 * CHALO)]
            grad[frame] = rows.reshape(-1, CH).astype(F32)

    width = (OWN + 2) * COLS
    own_cells = OWN * COLS

    def set_delta(l, t, value, to):
        cells = value.shape[0]
        valid = inside(first - l, OWN + 2 * l, total)
        delta = jnp.where(valid, value, 0.0).astype(BF16)
        at = HID + t * own_cells
        part[l, at : at + own_cells] = delta[l * COLS : l * COLS + own_cells]
        if l > 0:
            for lag_c, v in enumerate(shifted(delta.astype(F32))):
                to[t * 3 + lag_c, :cells] = v

    for l in range(LAYERS):
        rows = span - 2 * (l + 1)
        cells = rows * COLS
        src, dst = cols.at[l % 2], cols.at[(l + 1) % 2]
        for t in range(FR):
            at = (6 - l) * COLS
            part[l, t * width : (t + 1) * width] = src[t * 3 + 1, at : at + width]
        if l > 0:
            for k in range(TAPS):
                at = l * step + PLANE + (TAPS - 1 - k) * CH
                to = (l - 1) * step + PLANE + k * CH
                wb[to : to + CH] = wz[at : at + CH].T
        keep = slice((6 - 2 * l) * COLS, 10 * COLS)
        kept = (OWN + 2 * l) * COLS
        valid = inside(first - HALO + l + 1, rows, total)
        for p in range(FR // 2):
            lo = max(0, 2 * p - 2)
            pre2 = jnp.dot(
                taps_of(src, range(lo, 2 * p + 2), cells),
                pair_kernel(wz, l * step, 0 if p else 2),
                preferred_element_type=F32,
            )
            for e in range(2):
                t = 2 * p + e
                pre = pre2[:, e * CH : (e + 1) * CH]
                s = jax.nn.sigmoid(pre)
                if l + 1 < LAYERS:
                    new = src[t * 3 + 1, COLS : COLS + cells].astype(F32) + pre * s
                    new = jnp.where(valid, new, 0.0).astype(BF16).astype(F32)
                    for lag_c, v in enumerate(shifted(new)):
                        dst[t * 3 + lag_c, :cells] = v
                s, pre = s[keep], pre[keep]
                slope = s * (1.0 + pre * (1.0 - s))
                if l + 1 < LAYERS:
                    fac[l, t, :kept] = slope
                else:
                    set_delta(l, t, grad[t] * slope, dst)

    for l in reversed(range(1, LAYERS)):
        cells = (OWN + 2 * (l - 1)) * COLS
        src, dst = cols.at[(l + 1) % 2], cols.at[l % 2]
        for pairs in ((0, 1, 2), (3,)):
            hi = 4 if len(pairs) > 1 else 2
            lhs = [taps_of(src, range(2 * p, 2 * p + hi), cells) for p in pairs]
            kernel = pair_kernel(wb, (l - 1) * step, 0)[: hi * PLANE]
            adjoint = jnp.dot(jnp.concatenate(lhs, 0), kernel, preferred_element_type=F32)
            for i, p in enumerate(pairs):
                for e in range(2):
                    t = 2 * p + e
                    mine_of = adjoint[i * cells : (i + 1) * cells, e * CH : (e + 1) * CH]
                    new = grad[t, COLS : COLS + cells] + mine_of
                    new = new.astype(BF16).astype(F32)
                    if l > 1:
                        grad[t, :cells] = new
                    set_delta(l - 1, t, new * fac[l - 1, t, :cells], dst)


def kernel_grad_kernel(pos, parts, keep, send, cols, deltas, wg):
    tm = pos[1]
    cells = OWN * COLS
    width = cells + 2 * COLS
    total = LAYERS * FR * cells
    for m in range(LAYERS):
        e = parts.at[m]
        for t in range(FR):
            frame = e[t * width : (t + 1) * width]
            before, _, after = shifted(frame.astype(F32))
            for lag_c, v in enumerate((before, frame, after)):
                cols[lag_c, m * FR + t] = v
            deltas[m, t] = e[HID + t * cells : HID + (t + 1) * cells]
        for t in (FR, FR + 1):
            deltas[m, t] = jnp.zeros((cells, CH), BF16)
    x9 = jnp.concatenate(
        [
            cols[lag_c, :, lag_r * COLS : lag_r * COLS + cells].reshape(total, CH)
            for lag_r in range(3)
            for lag_c in range(3)
        ],
        1,
    )
    d3 = jnp.concatenate(
        [deltas[:, 2 - lag_t : 2 - lag_t + FR].reshape(total, CH) for lag_t in range(3)], 1
    )
    out = lax.dot_general(d3, x9, (((0,), (0,)), ((), ())), preferred_element_type=F32)
    for lag_t in range(3):
        for tap in range(9):
            at = (lag_t * 9 + tap) * CH
            wg[at : at + CH] = out[lag_t * CH : (lag_t + 1) * CH, tap * CH : (tap + 1) * CH].T
    keep[...] = wg[pl.ds(pl.multiple_of(tm * HALF, CH // 2), HALF)]
    send[...] = wg[pl.ds(pl.multiple_of((1 - tm) * HALF, CH // 2), HALF)].astype(BF16)


def zero_kernel(*refs):
    refs[-1][0] = 0


def zero_after(*arrays):
    return pl.pallas_call(
        zero_kernel,
        out_shape=jax.ShapeDtypeStruct((1,), jnp.int32),
        in_specs=[pl.BlockSpec(memory_space=pltpu.VMEM)] * len(arrays),
        out_specs=pl.BlockSpec(memory_space=pltpu.SMEM),
        compiler_params=pltpu.CompilerParams(vmem_limit_bytes=4 * 2**20),
        name="zero_after",
    )(*arrays)


def join_kernel(start, before, after, x, c, out):
    at = start[0]
    rows = x.shape[1]
    for t in range(FR // 2):
        for to, n, ref, lo in (
            (0, HALO, before, 0),
            (HALO, rows, x, 0),
            (HALO + rows, HALO, after, 0),
            (2 * HALO + rows, CHALO, before, HALO),
            (2 * HALO + CHALO + rows, rows, c, 0),
            (2 * HALO + CHALO + 2 * rows, CHALO, after, HALO),
        ):
            out[t, pl.ds(at + to, n)] = ref[t, lo : lo + n]


def run_join(start, *arrays):
    return pl.pallas_call(
        join_kernel,
        out_shape=jax.ShapeDtypeStruct((FR // 2, 4 * OWN + 2 * HALO + 2 * CHALO, COLS, CH), BF16),
        in_specs=in_vmem(4),
        out_specs=pl.BlockSpec(memory_space=pltpu.VMEM),
        compiler_params=pltpu.CompilerParams(vmem_limit_bytes=8 * 2**20),
        name="join",
    )(start, *arrays)


def in_vmem(n):
    return [pl.BlockSpec(memory_space=pltpu.SMEM)] + [pl.BlockSpec(memory_space=pltpu.VMEM)] * n


def run_layers(total, pos, *arrays):
    span = OWN + 2 * HALO
    return pl.pallas_call(
        functools.partial(layers_kernel, total),
        out_shape=jax.ShapeDtypeStruct((LAYERS, PART, CH), BF16),
        in_specs=in_vmem(len(arrays)),
        out_specs=pl.BlockSpec(memory_space=pltpu.VMEM),
        scratch_shapes=[
            pltpu.VMEM((PLANE + LAYERS * (PLANE + KC), CH), BF16),
            pltpu.VMEM((PLANE + (LAYERS - 1) * (PLANE + KC), CH), BF16),
            pltpu.VMEM((2, FR * 3, span * COLS, CH), BF16),
            pltpu.VMEM((LAYERS - 1, FR, (OWN + 2 * CHALO) * COLS, CH), F32),
            pltpu.VMEM((FR, (OWN + 2 * CHALO) * COLS, CH), F32),
        ],
        compiler_params=pltpu.CompilerParams(vmem_limit_bytes=28 * 2**20),
        cost_estimate=pl.CostEstimate(
            flops=9_000_000_000, bytes_accessed=6_000_000, transcendentals=1_000_000
        ),
        name="layers",
    )(pos, *arrays)


def run_kernel_grad(pos, *arrays):
    return pl.pallas_call(
        kernel_grad_kernel,
        out_shape=(
            jax.ShapeDtypeStruct((HALF, CH), F32),
            jax.ShapeDtypeStruct((HALF, CH), BF16),
        ),
        in_specs=in_vmem(len(arrays)),
        out_specs=(pl.BlockSpec(memory_space=pltpu.VMEM),) * 2,
        scratch_shapes=[
            pltpu.VMEM((3, LAYERS * FR, (OWN + 2) * COLS, CH), BF16),
            pltpu.VMEM((LAYERS, FR + 2, OWN * COLS, CH), BF16),
            pltpu.VMEM((KC, CH), F32),
        ],
        compiler_params=pltpu.CompilerParams(vmem_limit_bytes=24 * 2**20),
        cost_estimate=pl.CostEstimate(
            flops=1_800_000_000, bytes_accessed=4_000_000, transcendentals=0
        ),
        name="kernel_grad",
    )(pos, *arrays)


def ring(count, by):
    return [(i, (i + by) % count) for i in range(count)]


def along(x, by):
    return lax.ppermute(x, "segment", ring(LAYERS, by))


def swap(x):
    return lax.ppermute(x, "tm", [(0, 1), (1, 0)])


def body(inputs, weights, cotangent):
    seg, tm = lax.axis_index("segment"), lax.axis_index("tm")
    space = lax.axis_index(("z", "y"))
    spaces = lax.axis_size(("z", "y"))
    ny, nz = lax.axis_size("y"), lax.axis_size("z")
    rows = inputs.shape[2]
    pos = jnp.stack([seg, tm, space * rows + tm * OWN]).astype(jnp.int32)

    w = weights[0]
    half = lax.dynamic_slice_in_dim(w, tm * HALF, HALF, 0)
    left, right = along(half, 1), along(half, -1)
    got = [left, right, along(left[: HALF // 2], 1), along(right[HALF // 2 :], -1)]
    start = zero_after(*got[2:])
    crossed = [swap(g) for g in got]

    x = lax.dynamic_index_in_dim(inputs, seg, 0, keepdims=False)
    c = lax.dynamic_index_in_dim(cotangent, seg, 0, keepdims=False)
    down = [(i, i + 1) for i in range(spaces - 1)]
    up = [(i + 1, i) for i in range(spaces - 1)]
    before = lax.ppermute(
        jnp.concatenate([x[:, rows - HALO :], c[:, rows - CHALO :]], 1), ("z", "y"), down
    )
    after = lax.ppermute(jnp.concatenate([x[:, :HALO], c[:, :CHALO]], 1), ("z", "y"), up)
    mine = run_join(start, before, after, x, c)
    other = swap(mine)

    parts = run_layers(spaces * rows, pos, mine, other, w, *got, *crossed)
    parts = lax.all_to_all(parts, "segment", 0, 0)
    keep, send = run_kernel_grad(pos, parts)

    total = (keep + swap(send).astype(F32)).astype(BF16)
    rows_y = HALF // ny
    pieces = lax.all_to_all(total.reshape(ny, rows_y, CH), "y", 0, 0)
    total = jnp.sum(pieces.astype(F32), 0).astype(BF16)
    rows_z = -(-rows_y // (16 * nz)) * 16
    total = jnp.pad(total, ((0, nz * rows_z - rows_y), (0, 0)))
    pieces = lax.all_to_all(total.reshape(nz, rows_z, CH), "z", 0, 0)
    total = jnp.sum(pieces.astype(F32), 0).astype(BF16)
    whole = lax.all_to_all(jnp.broadcast_to(total, (nz, rows_z, CH)), "z", 0, 0)
    whole = whole.reshape(nz * rows_z, CH)[:rows_y]
    whole = lax.all_to_all(jnp.broadcast_to(whole, (ny, rows_y, CH)), "y", 0, 0)
    whole = whole.reshape(HALF, CH)
    theirs = swap(whole)
    low = jnp.where(tm == 0, whole, theirs)
    high = jnp.where(tm == 0, theirs, whole)
    return jnp.concatenate([low, high], 0).astype(F32)[None]


def solution(mesh):
    segments, cores, spaces = mesh.devices.shape
    ny = 4 if spaces % 4 == 0 else 1
    fine = Mesh(
        mesh.devices.reshape(segments, cores, spaces // ny, ny), ("segment", "tm", "z", "y")
    )
    spec = P(None, "tm", ("z", "y"), None, None)
    return jax.shard_map(
        body,
        mesh=fine,
        in_specs=(spec, P("segment", None, None), spec),
        out_specs=P("segment", None, None),
        check_vma=False,
    )
```

```python
import functools

import jax
import jax.numpy as jnp
from jax import lax
from jax.experimental import pallas as pl
from jax.experimental.pallas import tpu as pltpu
from jax.sharding import Mesh
from jax.sharding import PartitionSpec as P

BF16 = jnp.bfloat16
F32 = jnp.float32
CH = 128
COLS = 16
FR = 8
LAYERS = 4
TAPS = 27
KC = TAPS * CH
HALF = KC // 2
PLANE = 9 * CH
OWN = 4
HALO = 7
CHALO = 3
HID = FR * (OWN + 2) * COLS
PART = HID + FR * OWN * COLS


def shifted(x):
    cells = x.shape[0]
    col = lax.broadcasted_iota(jnp.int32, x.shape, 0) % COLS
    before = jnp.where(col == 0, 0.0, pltpu.roll(x, 1, 0))
    after = jnp.where(col == COLS - 1, 0.0, pltpu.roll(x, cells - 1, 0))
    return before.astype(BF16), x.astype(BF16), after.astype(BF16)


def inside(first, rows, total):
    row = first + lax.broadcasted_iota(jnp.int32, (rows * COLS, CH), 0) // COLS
    return (row >= 0) & (row < total)


def taps_of(cols, frames, cells):
    return jnp.concatenate(
        [
            cols[t * 3 + lag_c, lag_r * COLS : lag_r * COLS + cells]
            for t in frames
            for lag_r in range(3)
            for lag_c in range(3)
        ],
        1,
    )


def pair_kernel(ref, base, first):
    rows = (4 - first) * PLANE
    at = base + first * PLANE
    return jnp.concatenate(
        [ref[pl.ds(at + PLANE, rows)], ref[pl.ds(at, rows)]],
        1,
    )


def layers_kernel(
    total, pos, mine, other, w0, r1, r3, ra, rb, q1, q3, qa, qb, *rest
):
    o0, o1, oa, ob, o3, wz, wb, cols, fac, grad, part = rest
    seg, tm, first = pos[0], pos[1], pos[2]
    step = PLANE + KC
    zero = jnp.zeros((PLANE, CH), BF16)
    for l in range(LAYERS + 1):
        wz[l * step : l * step + PLANE] = zero
    for l in range(LAYERS):
        wb[l * step : l * step + PLANE] = zero
    wz[pl.ds(pl.multiple_of(seg * step + PLANE, CH), KC)] = w0[...]
    for d, skip, r, q in ((1, 0, r1, q1), (3, 0, r3, q3), (2, 0, ra, qa), (2, HALF // 2, rb, qb)):
        at = lax.rem(seg + LAYERS - d, LAYERS) * step + PLANE + skip
        for ref, half in ((r, tm), (q, 1 - tm)):
            wz[pl.ds(pl.multiple_of(at + half * HALF, 32), ref.shape[0])] = ref[...]

    span = OWN + 2 * HALO
    half_fr = FR // 2
    for ref, which in ((mine, tm), (other, 1 - tm)):

        @pl.loop(0, half_fr)
        def _(t):
            frame = which * half_fr + t
            rows = ref[t, pl.ds(tm * OWN, span)]
            for lag_c, v in enumerate(shifted(rows.reshape(span * COLS, CH).astype(F32))):
                cols[0, frame * 3 + lag_c] = v
            at = 2 * HALO + 2 * OWN + tm * OWN
            rows = ref[t, pl.ds(at, OWN + 2 * CHALO)]
            grad[frame] = rows.reshape(-1, CH).astype(F32)

    width = (OWN + 2) * COLS
    own_cells = OWN * COLS

    def set_delta(l, t, value, to):
        cells = value.shape[0]
        valid = inside(first - l, OWN + 2 * l, total)
        delta = jnp.where(valid, value, 0.0).astype(BF16)
        at = HID + t * own_cells
        part[l, at : at + own_cells] = delta[l * COLS : l * COLS + own_cells]
        if l > 0:
            for lag_c, v in enumerate(shifted(delta.astype(F32))):
                to[t * 3 + lag_c, :cells] = v

    for l in range(LAYERS):
        rows = span - 2 * (l + 1)
        cells = rows * COLS
        src, dst = cols.at[l % 2], cols.at[(l + 1) % 2]
        for t in range(FR):
            at = (6 - l) * COLS
            part[l, t * width : (t + 1) * width] = src[t * 3 + 1, at : at + width]
        if l > 0:
            for k in range(TAPS):
                at = l * step + PLANE + (TAPS - 1 - k) * CH
                to = (l - 1) * step + PLANE + k * CH
                wb[to : to + CH] = wz[at : at + CH].T
        keep = slice((6 - 2 * l) * COLS, 10 * COLS)
        kept = (OWN + 2 * l) * COLS
        valid = inside(first - HALO + l + 1, rows, total)
        for p in range(FR // 2):
            lo = max(0, 2 * p - 2)
            pre2 = jnp.dot(
                taps_of(src, range(lo, 2 * p + 2), cells),
                pair_kernel(wz, l * step, 0 if p else 2),
                preferred_element_type=F32,
            )
            for e in range(2):
                t = 2 * p + e
                pre = pre2[:, e * CH : (e + 1) * CH]
                s = jax.nn.sigmoid(pre)
                if l + 1 < LAYERS:
                    new = src[t * 3 + 1, COLS : COLS + cells].astype(F32) + pre * s
                    new = jnp.where(valid, new, 0.0).astype(BF16).astype(F32)
                    for lag_c, v in enumerate(shifted(new)):
                        dst[t * 3 + lag_c, :cells] = v
                s, pre = s[keep], pre[keep]
                slope = s * (1.0 + pre * (1.0 - s))
                if l + 1 < LAYERS:
                    fac[l, t, :kept] = slope
                else:
                    set_delta(l, t, grad[t] * slope, dst)

    for l in reversed(range(1, LAYERS)):
        cells = (OWN + 2 * (l - 1)) * COLS
        src, dst = cols.at[(l + 1) % 2], cols.at[l % 2]
        for pairs in ((0, 1, 2), (3,)):
            hi = 4 if len(pairs) > 1 else 2
            lhs = [taps_of(src, range(2 * p, 2 * p + hi), cells) for p in pairs]
            kernel = pair_kernel(wb, (l - 1) * step, 0)[: hi * PLANE]
            adjoint = jnp.dot(jnp.concatenate(lhs, 0), kernel, preferred_element_type=F32)
            for i, p in enumerate(pairs):
                for e in range(2):
                    t = 2 * p + e
                    mine_of = adjoint[i * cells : (i + 1) * cells, e * CH : (e + 1) * CH]
                    new = grad[t, COLS : COLS + cells] + mine_of
                    new = new.astype(BF16).astype(F32)
                    if l > 1:
                        grad[t, :cells] = new
                    set_delta(l - 1, t, new * fac[l - 1, t, :cells], dst)

    for d, lo, out in ((0, 0, o0), (1, 0, o1), (2, 0, oa), (2, PART // 2, ob), (3, 0, o3)):
        out[...] = part[lax.rem(seg + d, LAYERS), lo : lo + out.shape[0]]


def kernel_grad_kernel(pos, e0, e1, e3, ea, eb, keep, send, e2, cols, deltas, wg):
    tm = pos[1]
    e2[: PART // 2] = ea[...]
    e2[PART // 2 :] = eb[...]
    cells = OWN * COLS
    width = cells + 2 * COLS
    total = LAYERS * FR * cells
    for m, e in enumerate((e0, e1, e2, e3)):
        for t in range(FR):
            frame = e[t * width : (t + 1) * width]
            before, _, after = shifted(frame.astype(F32))
            for lag_c, v in enumerate((before, frame, after)):
                cols[lag_c, m * FR + t] = v
            deltas[m, t] = e[HID + t * cells : HID + (t + 1) * cells]
        for t in (FR, FR + 1):
            deltas[m, t] = jnp.zeros((cells, CH), BF16)
    x9 = jnp.concatenate(
        [
            cols[lag_c, :, lag_r * COLS : lag_r * COLS + cells].reshape(total, CH)
            for lag_r in range(3)
            for lag_c in range(3)
        ],
        1,
    )
    d3 = jnp.concatenate(
        [deltas[:, 2 - lag_t : 2 - lag_t + FR].reshape(total, CH) for lag_t in range(3)], 1
    )
    out = lax.dot_general(d3, x9, (((0,), (0,)), ((), ())), preferred_element_type=F32)
    for lag_t in range(3):
        for tap in range(9):
            at = (lag_t * 9 + tap) * CH
            wg[at : at + CH] = out[lag_t * CH : (lag_t + 1) * CH, tap * CH : (tap + 1) * CH].T
    keep[...] = wg[pl.ds(pl.multiple_of(tm * HALF, CH // 2), HALF)]
    send[...] = wg[pl.ds(pl.multiple_of((1 - tm) * HALF, CH // 2), HALF)].astype(BF16)


def in_vmem(n):
    return [pl.BlockSpec(memory_space=pltpu.SMEM)] + [pl.BlockSpec(memory_space=pltpu.VMEM)] * n


def run_layers(total, pos, *arrays):
    span = OWN + 2 * HALO
    lengths = (PART, PART, PART // 2, PART // 2, PART)
    return pl.pallas_call(
        functools.partial(layers_kernel, total),
        out_shape=tuple(jax.ShapeDtypeStruct((n, CH), BF16) for n in lengths),
        in_specs=in_vmem(len(arrays)),
        out_specs=(pl.BlockSpec(memory_space=pltpu.VMEM),) * len(lengths),
        scratch_shapes=[
            pltpu.VMEM((PLANE + LAYERS * (PLANE + KC), CH), BF16),
            pltpu.VMEM((PLANE + (LAYERS - 1) * (PLANE + KC), CH), BF16),
            pltpu.VMEM((2, FR * 3, span * COLS, CH), BF16),
            pltpu.VMEM((LAYERS - 1, FR, (OWN + 2 * CHALO) * COLS, CH), F32),
            pltpu.VMEM((FR, (OWN + 2 * CHALO) * COLS, CH), F32),
            pltpu.VMEM((LAYERS, PART, CH), BF16),
        ],
        compiler_params=pltpu.CompilerParams(vmem_limit_bytes=44 * 2**20),
        cost_estimate=pl.CostEstimate(
            flops=9_000_000_000, bytes_accessed=6_000_000, transcendentals=1_000_000
        ),
        name="layers",
    )(pos, *arrays)


def run_kernel_grad(pos, *arrays):
    return pl.pallas_call(
        kernel_grad_kernel,
        out_shape=(
            jax.ShapeDtypeStruct((HALF, CH), F32),
            jax.ShapeDtypeStruct((HALF, CH), BF16),
        ),
        in_specs=in_vmem(len(arrays)),
        out_specs=(pl.BlockSpec(memory_space=pltpu.VMEM),) * 2,
        scratch_shapes=[
            pltpu.VMEM((PART, CH), BF16),
            pltpu.VMEM((3, LAYERS * FR, (OWN + 2) * COLS, CH), BF16),
            pltpu.VMEM((LAYERS, FR + 2, OWN * COLS, CH), BF16),
            pltpu.VMEM((KC, CH), F32),
        ],
        compiler_params=pltpu.CompilerParams(vmem_limit_bytes=32 * 2**20),
        cost_estimate=pl.CostEstimate(
            flops=1_800_000_000, bytes_accessed=4_000_000, transcendentals=0
        ),
        name="kernel_grad",
    )(pos, *arrays)


def ring(count, by):
    return [(i, (i + by) % count) for i in range(count)]


def along(x, by):
    return lax.ppermute(x, "segment", ring(LAYERS, by))


def swap(x):
    return lax.ppermute(x, "tm", [(0, 1), (1, 0)])


def body(inputs, weights, cotangent):
    seg, tm = lax.axis_index("segment"), lax.axis_index("tm")
    space = lax.axis_index(("z", "y"))
    spaces = lax.axis_size(("z", "y"))
    ny, nz = lax.axis_size("y"), lax.axis_size("z")
    rows = inputs.shape[2]
    pos = jnp.stack([seg, tm, space * rows + tm * OWN]).astype(jnp.int32)

    w = weights[0]
    half = lax.dynamic_slice_in_dim(w, tm * HALF, HALF, 0)
    left, right = along(half, 1), along(half, -1)
    got = [left, right, along(left[: HALF // 2], 1), along(right[HALF // 2 :], -1)]
    crossed = [swap(g) for g in got]

    x = lax.dynamic_index_in_dim(inputs, seg, 0, keepdims=False)
    c = lax.dynamic_index_in_dim(cotangent, seg, 0, keepdims=False)
    down = [(i, i + 1) for i in range(spaces - 1)]
    up = [(i + 1, i) for i in range(spaces - 1)]
    before = lax.ppermute(
        jnp.concatenate([x[:, rows - HALO :], c[:, rows - CHALO :]], 1), ("z", "y"), down
    )
    after = lax.ppermute(jnp.concatenate([x[:, :HALO], c[:, :CHALO]], 1), ("z", "y"), up)
    mine = jnp.concatenate(
        [before[:, :HALO], x, after[:, :HALO], before[:, HALO:], c, after[:, HALO:]], 1
    )
    other = swap(mine)

    parts = run_layers(spaces * rows, pos, mine, other, w, *got, *crossed)
    far_a, far_b = along(parts[2], 1), along(parts[3], -1)
    near = [along(parts[1], 1), along(parts[4], -1)]
    keep, send = run_kernel_grad(pos, parts[0], *near, along(far_a, 1), along(far_b, -1))

    total = (keep + swap(send).astype(F32)).astype(BF16)
    rows_y = HALF // ny
    pieces = lax.all_to_all(total.reshape(ny, rows_y, CH), "y", 0, 0)
    total = jnp.sum(pieces.astype(F32), 0).astype(BF16)
    rows_z = -(-rows_y // (16 * nz)) * 16
    total = jnp.pad(total, ((0, nz * rows_z - rows_y), (0, 0)))
    pieces = lax.all_to_all(total.reshape(nz, rows_z, CH), "z", 0, 0)
    total = jnp.sum(pieces.astype(F32), 0).astype(BF16)
    whole = lax.all_to_all(jnp.broadcast_to(total, (nz, rows_z, CH)), "z", 0, 0)
    whole = whole.reshape(nz * rows_z, CH)[:rows_y]
    whole = lax.all_to_all(jnp.broadcast_to(whole, (ny, rows_y, CH)), "y", 0, 0)
    whole = whole.reshape(HALF, CH)
    theirs = swap(whole)
    low = jnp.where(tm == 0, whole, theirs)
    high = jnp.where(tm == 0, theirs, whole)
    return jnp.concatenate([low, high], 0).astype(F32)[None]


def solution(mesh):
    segments, cores, spaces = mesh.devices.shape
    ny = 4 if spaces % 4 == 0 else 1
    fine = Mesh(
        mesh.devices.reshape(segments, cores, spaces // ny, ny), ("segment", "tm", "z", "y")
    )
    spec = P(None, "tm", ("z", "y"), None, None)
    return jax.shard_map(
        body,
        mesh=fine,
        in_specs=(spec, P("segment", None, None), spec),
        out_specs=P("segment", None, None),
        check_vma=False,
    )
```
